512 devices in a mesh: gz: 8 (over y), gx: 32 (over x, z), gy: 2 (over core).
Axes of the slice: x: 4, y: 8, z: 8, core: 2. Of those that a mesh axis runs over, the one named last changes fastest.
Arguments:
- electron_density: float32 [128, 512, 512], P('gz', 'gx', 'gy'), may hold values from 0.1 to 4
- hole_density: float32 [128, 512, 512], P('gz', 'gx', 'gy'), may hold values from 0.1 to 4
- potential: float32 [128, 512, 512], P('gz', 'gx', 'gy'), may hold values from -6 to 6
- doping: float32 [128, 512, 512], P('gz', 'gx', 'gy'), may hold values from -6 to 6
- electron_mobility: float32 [128, 512, 512], P('gz', 'gx', 'gy'), may hold values from 0.02 to 0.16
- hole_mobility: float32 [128, 512, 512], P('gz', 'gx', 'gy'), may hold values from 0.02 to 0.16
- cfl_map: int32 [512, 512], P('gx', 'gy'), may hold values from 0 to 8
- fraction: float32 [512, 512], P('gx', 'gy'), may hold values from 0 to 1
Outputs:
- negative_concentration_next: float32 [128, 512, 512], P('gz', 'gx', 'gy')
- positive_concentration_next: float32 [128, 512, 512], P('gz', 'gx', 'gy')
- potential_field: float32 [128, 512, 512], P('gz', 'gx', 'gy')
The draws below stay inside these ranges and needn't reach their ends.
All inputs are finite; a program needn't handle non-finite values.
Results may differ from the reference program's by a relative error of at most 0.00002.
Values sent between devices are 32-bit elements; how exact they have to be, the bound alone decides.
A program may use at most 128 MiB of HBM per device.

```python
import math
import jax
import jax.numpy as jnp

CFL_MAX = 8
DIFFUSION_SWEEPS = 2
JACOBI_SWEEPS = 4
NZ = 128
NX = 512
NY = 512


def plant(entries, key, least, largest):
    longest = entries.shape.index(max(entries.shape))
    spots = []
    for shift in (0, 1):
        where = [jax.random.randint(jax.random.fold_in(key, axis), (), 0, length) for axis, length in enumerate(entries.shape)]
        where[longest] = (where[longest] + shift) % entries.shape[longest]
        spots.append(tuple(where))
    return entries.at[spots[0]].set(least).at[spots[1]].set(largest)


def shard_levels(key, extent, pieces, least, largest):
    gain, own = 1.0, jax.random.fold_in(key, 6)
    for position, shards_of in pieces:
        steps = jnp.exp(jax.random.uniform(jax.random.fold_in(own, position), (shards_of,), jnp.float32, least / len(pieces), largest / len(pieces)))
        gain = gain * jnp.repeat(steps, extent[position] // shards_of).reshape([-1 if axis == position else 1 for axis in range(len(extent))])
    return gain


def bell_draw(key, extent, deviation, limit, pieces=(), dtype=jnp.bfloat16):
    array = jax.random.normal(key, extent, jnp.float32) * deviation
    if len(pieces) > 0:
        array = shard_levels(key, extent, pieces, -0.22, 0.18) * array
    return jnp.clip(array, min=-limit, max=limit).astype(dtype)


def setup_inputs(seed: int = 0) -> dict:
    key_list = jax.random.split(jax.random.key(seed), 9)
    return {
        "electron_density": jnp.clip(jnp.exp(math.log(4.0) - 3.6888794 * jax.random.uniform(key_list[0], (NZ, NX, NY), jnp.float32) ** shard_levels(key_list[0], (NZ, NX, NY), ((0, 8), (1, 32), (2, 2)), -0.2, 0.2)), 0.1, 4.0),
        "hole_density": jnp.clip(jnp.exp(math.log(4.0) - 3.6888794 * jax.random.uniform(key_list[1], (NZ, NX, NY), jnp.float32) ** shard_levels(key_list[1], (NZ, NX, NY), ((0, 8), (1, 32), (2, 2)), -0.2, 0.2)), 0.1, 4.0),
        "potential": bell_draw(key_list[2], (NZ, NX, NY), 1.0, 6.0, ((0, 8), (1, 32), (2, 2)), jnp.float32),
        "doping": bell_draw(key_list[3], (NZ, NX, NY), 1.0, 6.0, ((0, 8), (1, 32), (2, 2)), jnp.float32),
        "electron_mobility": jnp.clip(jnp.exp(math.log(0.16) - 2.0794415 * jax.random.uniform(key_list[4], (NZ, NX, NY), jnp.float32) ** shard_levels(key_list[4], (NZ, NX, NY), ((0, 8), (1, 32), (2, 2)), -0.2, 0.2)), 0.02, 0.16),
        "hole_mobility": jnp.clip(jnp.exp(math.log(0.16) - 2.0794415 * jax.random.uniform(key_list[5], (NZ, NX, NY), jnp.float32) ** shard_levels(key_list[5], (NZ, NX, NY), ((0, 8), (1, 32), (2, 2)), -0.2, 0.2)), 0.02, 0.16),
        "cfl_map": plant(jax.random.randint(key_list[6], (NX, NY), 0, CFL_MAX + 1), jax.random.fold_in(key_list[6], 1), 0, CFL_MAX).astype(jnp.int32),
        "fraction": jnp.clip(1.0 * jax.random.uniform(key_list[7], (NX, NY), jnp.float32) ** shard_levels(key_list[7], (NX, NY), ((0, 32), (1, 2)), -0.2, 0.2), 0.0, 1.0),
    }


def neighbours(enlarged_mesh):
    return [enlarged_mesh[..., 2:, 1:-1, 1:-1], enlarged_mesh[..., :-2, 1:-1, 1:-1], enlarged_mesh[..., 1:-1, 2:, 1:-1], enlarged_mesh[..., 1:-1, :-2, 1:-1], enlarged_mesh[..., 1:-1, 1:-1, 2:], enlarged_mesh[..., 1:-1, 1:-1, :-2]]

def upstream(enlarged_mesh, anchor, orient, cfl_map, fraction, layers):
    summed = jnp.zeros((layers,) + cfl_map.shape, jnp.float32)
    for reach_k in range(CFL_MAX + 2):
        weights = jnp.where(cfl_map == reach_k, 1.0 - fraction, 0.0) + jnp.where(cfl_map + 1 == reach_k, fraction, 0.0)
        offset = anchor + orient * reach_k
        summed = summed + weights[None] * enlarged_mesh[offset:offset + layers]
    return summed

def spread_by_gradient(enlarged_mesh, particle_kinds, linking_factors):
    nearby_sites_list = neighbours(enlarged_mesh)
    concentration_change = linking_factors[0] * (nearby_sites_list[0] - particle_kinds)
    for junction_position in range(1, 6):
        concentration_change = concentration_change + linking_factors[junction_position] * (nearby_sites_list[junction_position] - particle_kinds)
    return particle_kinds + concentration_change

def relax(enlarged_mesh, charge):
    nearby_sites_list = neighbours(enlarged_mesh)
    summed = nearby_sites_list[0] + nearby_sites_list[1] + nearby_sites_list[2] + nearby_sites_list[3] + nearby_sites_list[4] + nearby_sites_list[5]
    return (summed + charge) / 6.0

def bordered_planes(values):
    return jnp.pad(values, ((0, 0), (1, 1), (1, 1), (1, 1)))

def reference(electron_density, hole_density, potential, doping, electron_mobility, hole_mobility, cfl_map, fraction):
    layers = electron_density.shape[0]
    margin = CFL_MAX + 1
    padded_e = jnp.pad(electron_density, ((margin, margin), (0, 0), (0, 0)))
    padded_h = jnp.pad(hole_density, ((margin, margin), (0, 0), (0, 0)))
    transported_negative_charges = upstream(padded_e, margin, -1, cfl_map, fraction, layers)
    transported_positive_charges = upstream(padded_h, margin, 1, cfl_map, fraction, layers)
    mobility = bordered_planes(jnp.stack([electron_mobility, hole_mobility]))
    middle = mobility[:, 1:-1, 1:-1, 1:-1]
    linking_factors = [jnp.sqrt(middle * nearby_sites_list) for nearby_sites_list in neighbours(mobility)]
    particle_kinds = jnp.stack([transported_negative_charges, transported_positive_charges])
    for sweep_index in range(DIFFUSION_SWEEPS):
        particle_kinds = spread_by_gradient(bordered_planes(particle_kinds), particle_kinds, linking_factors)
    negative_concentration_next = particle_kinds[0]
    positive_concentration_next = particle_kinds[1]
    charge = 0.5 * (positive_concentration_next - negative_concentration_next + doping)
    potential_field = potential
    for sweep_index in range(JACOBI_SWEEPS):
        potential_field = relax(jnp.pad(potential_field, 1), charge)
    return (negative_concentration_next, positive_concentration_next, potential_field)
```

```python
import jax
import jax.numpy as jnp
from jax import lax
from jax.experimental import pallas as pl
from jax.experimental.pallas import tpu as pltpu
from jax.sharding import PartitionSpec as P

MESH = pl.DeviceIdType.MESH

CFL_MAX = 8
NZ = 16
NR = 16
NL = 256
OWN = 8
OFF = 4
TILES = 4
ROWS = 24
TOP = 4
FIRST = TOP + OFF
SWEEP_HALO = 2
UP = CFL_MAX + 1 + SWEEP_HALO

E, H, ME, MH, PHI, DOP, CFL, FRAC = range(8)
REACH = {
    E: (2, UP, 2),
    H: (2, 2, UP),
    ME: (2, 2, 2),
    MH: (2, 2, 2),
    PHI: (4, 4, 4),
    DOP: (0, 0, 0),
    CFL: (2, 0, 0),
    FRAC: (2, 0, 0),
}
FLAT = (CFL, FRAC)


def received_rows(field):
    rows, below, above = REACH[field]
    if field in FLAT:
        return OWN + 2 * rows
    near = (NZ + below + above) * (OWN + rows)
    if rows == 0:
        return near
    return near + (NZ + below + above - 2) * rows


def sent_rows(field, dz):
    rows, below, above = REACH[field]
    if field in FLAT:
        return (OWN + rows) + 2 * rows if dz == 0 else 0
    if dz == 0:
        return NZ * (OWN + rows) + 2 * NZ * rows
    depth = below if dz == 1 else above
    if depth == 0:
        return 0
    return depth * 2 * (OWN + rows) + 2 * (depth - 1) * rows


def kernel(sizes, *refs):
    n_gz, n_gx = sizes
    ins = refs[:8]
    outs = refs[8:11]
    land = refs[11:19]
    (s_buf, rs_buf, a_buf, q0, q1, c_buf, v_a, v_b, u_a, u_b, stage, count, in_send, in_recv, c_send, c_recv, o_send,
     o_recv) = refs[19:]
    g, w, c = lax.axis_index("gz"), lax.axis_index("gx"), lax.axis_index("gy")

    def at(dz, dx, core):
        return (lax.rem(g + (dz + n_gz), n_gz), lax.rem(w + (dx + n_gx), n_gx), core)

    barrier = pltpu.get_barrier_semaphore()
    side = 2 * c - 1
    for dz in (0, 1, -1):
        if dz != 0:
            pl.semaphore_signal(barrier, inc=1, device_id=at(dz, 0, c), device_id_type=MESH)
        pl.semaphore_signal(barrier, inc=1, device_id=at(dz, 0, 1 - c), device_id_type=MESH)
        for core in (0, 1):
            pl.semaphore_signal(barrier, inc=1, device_id=at(dz, side, core), device_id_type=MESH)
    pl.semaphore_wait(barrier, 11)

    lanes = pl.ds(pl.multiple_of(c * NL, NL), NL)

    def push(field, dz, piece):
        if piece in (0, 1):
            move(field, dz, 0, piece, piece)
        elif piece == "right":
            move(field, dz, 1, 0, piece)
        else:
            move(field, dz, -1, 1, piece)

    def move(field, dz, dx, core, piece):
        rows, below, above = REACH[field]
        clip = abs(dx)
        depth = {0: NZ, 1: below - clip, -1: above - clip}[dz]
        if depth <= 0 or (rows == 0 and clip) or (field in FLAT and dz != 0):
            return
        pieces = {
            0: [(0, 0, OWN), (OWN, OWN, rows)],
            1: [(OWN, 0, OWN), (OWN - rows, NR - rows, rows)],
            "right": [(NR - rows, NR - rows, rows)],
            "left": [(0, OWN, rows)],
        }[piece]
        for src_x, dst_x, size in pieces:
            if size == 0:
                continue
            src_x, dst_x = pl.ds(src_x, size), pl.ds(dst_x, size)
            if field in FLAT:
                src, dst = ins[field].at[src_x, :], land[field].at[dst_x, lanes]
            else:
                src_z, dst_z = {0: (0, below), 1: (NZ - depth, below - depth), -1: (0, below + NZ)}[dz]
                src = ins[field].at[pl.ds(src_z, depth), src_x, :]
                dst = land[field].at[pl.ds(dst_z, depth), dst_x, lanes]
            send(field, dz, dx, core, src, dst)

    def send(field, dz, dx, core, src, dst):
        def remote():
            pltpu.make_async_remote_copy(
                src_ref=src,
                dst_ref=dst,
                send_sem=in_send.at[field, dz + 1],
                recv_sem=in_recv.at[field],
                device_id=at(dz, dx, core),
                device_id_type=MESH,
            ).start()

        if dz == 0 and dx == 0:

            @pl.when(c == core)
            def _():
                pltpu.make_async_copy(src, dst, in_recv.at[field]).start()

            @pl.when(c != core)
            def _():
                remote()
        else:
            remote()

    def arrived(field):
        view = count.at[pl.ds(0, TILES * received_rows(field)), :]
        pltpu.make_async_copy(view, view, in_recv.at[field]).wait()

    for field in (ME, MH):
        for dz in (1, -1):
            for piece in ("right", "left", 0, 1):
                push(field, dz, piece)
    for field, dz in ((E, 1), (H, -1)):
        for piece in ("right", "left"):
            push(field, dz, piece)
    for field, dz in ((E, 1), (H, -1)):
        for piece in (0, 1):
            push(field, dz, piece)
    for field in (ME, MH):
        for piece in ("right", "left", 0, 1):
            push(field, 0, piece)
    for field, dz in ((E, -1), (H, 1)):
        for piece in ("right", "left", 0, 1):
            push(field, dz, piece)
    for field in (E, H, CFL, FRAC):
        for piece in ("right", "left", 0, 1):
            push(field, 0, piece)
    for dz in (1, -1, 0):
        for piece in ("right", "left", 0, 1):
            push(PHI, dz, piece)
    for piece in (0, 1):
        push(DOP, 0, piece)

    row = lax.broadcasted_iota(jnp.int32, (NR, 128), 0)
    out_left = jnp.logical_and(w == 0, c == 0)
    out_right = jnp.logical_and(w == n_gx - 1, c == 1)
    first_row = jnp.where(out_left, OFF, 0)
    last_row = jnp.where(out_right, OFF + OWN, NR)
    inside = jnp.where(jnp.logical_and(row >= first_row, row < last_row), 1.0, 0.0)
    halo_row = lax.broadcasted_iota(jnp.int32, (8, 128), 0)
    halo_out = jnp.where(halo_row < OFF, jnp.where(out_right, 1, 0), jnp.where(out_left, 1, 0))
    halo_inside = jnp.where(halo_out == 0, 1.0, 0.0)
    lane = lax.broadcasted_iota(jnp.int32, (NR, 128), 1)
    at_first, at_last = lane == 0, lane == 127
    lo_end, hi_end = g == 0, g == n_gz - 1

    def layer_in(z, below):
        first = jnp.where(lo_end, below, 0)
        last = jnp.where(hi_end, below + NZ, below + NZ + below)
        return jnp.where(jnp.logical_and(z >= first, z < last), 1.0, 0.0)

    def around(ref, z, start, rows):
        centre = [ref[z, t, pl.ds(start, rows), :] for t in range(TILES)]
        up = [pltpu.roll(v, 127, 1) for v in centre] + [jnp.zeros((rows, 128), jnp.float32)]
        down = [jnp.zeros((rows, 128), jnp.float32)] + [pltpu.roll(v, 1, 1) for v in centre]
        is_first, is_last = at_first[:rows], at_last[:rows]
        sums = []
        for t in range(TILES):
            in_y = jnp.where(is_last, up[t + 1], up[t]) + jnp.where(is_first, down[t], down[t + 1])
            in_z = ref[z + 1, t, pl.ds(start, rows), :] + ref[z - 1, t, pl.ds(start, rows), :]
            in_x = ref[z, t, pl.ds(start + 1, rows), :] + ref[z, t, pl.ds(start - 1, rows), :]
            sums.append((in_z + in_x) + in_y)
        return centre, sums

    for kind, field in ((0, ME), (1, MH)):
        arrived(field)

        def roots(z, _, kind=kind, field=field):
            in_z = layer_in(z, SWEEP_HALO)
            halo_mask = halo_inside * in_z
            for t in range(TILES):
                m = land[field][z, pl.ds(0, OWN), pl.ds(128 * t, 128)]
                rs = lax.rsqrt(m)
                rs_buf[kind, z, t] = rs
                s_buf[kind, z, t, pl.ds(FIRST, OWN), :] = (m * rs) * in_z
                m = land[field][z, pl.ds(OWN, 8), pl.ds(128 * t, 128)]
                s = (m * lax.rsqrt(m)) * halo_mask
                s_buf[kind, z, t, pl.ds(0, 8), :] = s
                s_buf[kind, z, t, pl.ds(FIRST + OWN, 8), :] = s
            return 0

        lax.fori_loop(0, NZ + 2 * SWEEP_HALO, roots, 0, unroll=2)

    for kind in (0, 1):

        def stays(z, _, kind=kind):
            centre, sums = around(s_buf.at[kind], z, TOP, NR)
            for t in range(TILES):
                a_buf[kind, z, t, pl.ds(TOP, NR), :] = 1.0 - centre[t] * sums[t]
            return 0

        lax.fori_loop(1, NZ + 2 * SWEEP_HALO - 1, stays, 0, unroll=3)

    arrived(CFL)
    arrived(FRAC)
    arrived(E)
    arrived(H)

    @pl.when(lo_end)
    def _():
        for z in range(UP):
            land[E][z] = jnp.zeros((NR, 2 * NL), jnp.float32)

    @pl.when(hi_end)
    def _():
        for z in range(SWEEP_HALO + NZ, SWEEP_HALO + NZ + UP):
            land[H][z] = jnp.zeros((NR, 2 * NL), jnp.float32)

    layers = NZ + 2 * SWEEP_HALO
    for half in range(2):
        rows = pl.ds(8 * half, 8)
        target_rows = pl.ds(FIRST + 8 * half, 8)

        def drift(t, _, half=half, rows=rows, target_rows=target_rows):
            tile = pl.ds(pl.multiple_of(t * 128, 128), 128)
            d = land[CFL][rows, tile]
            f = land[FRAC][rows, tile]
            rest = 1.0 - f
            bits = [(k, jnp.bitwise_and(d, k) != 0) for k in (8, 4, 2, 1)]
            for kind, field in ((0, E), (1, H)):
                length = layers + UP - 2
                if kind == 0:
                    v = [land[field][length - 1 - i, rows, tile] for i in range(length)]
                else:
                    v = [land[field][i, rows, tile] for i in range(length)]
                for k, bit in bits:
                    if k == 8:
                        v = [jnp.where(bit, v[i + 8], v[i]) if i <= layers else v[i] for i in range(length - 1)]
                    else:
                        v = [jnp.where(bit, v[i + k], v[i]) for i in range(len(v) - k)]
                for i in range(layers):
                    z = layers - 1 - i if kind == 0 else i
                    n = rest * v[i] + f * v[i + 1]
                    q = n * s_buf[kind, z, t, target_rows, :]
                    q0[kind, z, t, target_rows, :] = q
                    if half == 1:
                        q0[kind, z, t, pl.ds(0, 8), :] = q
            return 0

        lax.fori_loop(0, TILES, drift, 0)

    def sweep_one(z, _):
        for kind in (0, 1):
            centre, sums = around(q0.at[kind], z, TOP, NR)
            for t in range(TILES):
                s = s_buf[kind, z, t, pl.ds(TOP, NR), :]
                q1[kind, z, t, pl.ds(TOP, NR), :] = centre[t] * a_buf[kind, z, t, pl.ds(TOP, NR), :] + (s * s) * sums[t]
        return 0

    lax.fori_loop(1, layers - 1, sweep_one, 0, unroll=2)

    arrived(DOP)
    own = pl.ds(FIRST, OWN)

    def sweep_two(z, _):
        found = []
        for kind in (0, 1):
            centre, sums = around(q1.at[kind], z + SWEEP_HALO, FIRST, OWN)
            n = []
            for t in range(TILES):
                s = s_buf[kind, z + SWEEP_HALO, t, own, :]
                q = centre[t] * a_buf[kind, z + SWEEP_HALO, t, own, :] + (s * s) * sums[t]
                n.append(q * rs_buf[kind, z + SWEEP_HALO, t])
                stage[kind, z, :, pl.ds(128 * t, 128)] = n[t]
            found.append(n)
        for t in range(TILES):
            doping = land[DOP][z, :, pl.ds(128 * t, 128)]
            c_buf[z + 3, t, own, :] = (found[1][t] - found[0][t] + doping) * (0.5 / 6.0)
        return 0

    lax.fori_loop(0, NZ, sweep_two, 0, unroll=2)

    copies = []

    def share(src, dst, target):
        k = len(copies)
        copy = pltpu.make_async_remote_copy(
            src_ref=src,
            dst_ref=dst,
            send_sem=c_send.at[k],
            recv_sem=c_recv.at[k],
            device_id=target,
            device_id_type=MESH,
        )
        copy.start()
        copies.append(copy)

    right_dx, left_dx = c, c - 1
    for src_z, dst_z, size, dz in ((3 + NZ - 2, 1, 2, 1), (3, 3 + NZ, 2, -1)):
        for dx, src_x, dst_x in ((right_dx, FIRST + OWN - 2, FIRST - 2), (left_dx, FIRST, FIRST + OWN)):
            share(
                c_buf.at[pl.ds(src_z, size), :, pl.ds(src_x, 2), :],
                c_buf.at[pl.ds(dst_z, size), :, pl.ds(dst_x, 2), :],
                at(dz, dx, 1 - c),
            )
    for dx, src_x, dst_x in ((right_dx, FIRST + OWN - 3, FIRST - 3), (left_dx, FIRST, FIRST + OWN)):
        share(
            c_buf.at[pl.ds(3, NZ), :, pl.ds(src_x, 3), :],
            c_buf.at[pl.ds(3, NZ), :, pl.ds(dst_x, 3), :],
            at(0, dx, 1 - c),
        )
    for src_z, dst_z, dz in ((NZ, 0, 1), (3, 3 + NZ, -1)):
        share(
            c_buf.at[pl.ds(src_z, 3), :, pl.ds(FIRST, OWN), :],
            c_buf.at[pl.ds(dst_z, 3), :, pl.ds(FIRST, OWN), :],
            at(dz, 0, c),
        )

    def give(index):
        mine = pl.ds(pl.multiple_of(c * OWN, OWN), OWN)
        others = pl.ds(pl.multiple_of((1 - c) * NL, NL), NL)
        pltpu.make_async_remote_copy(
            src_ref=stage.at[index, :, :, others],
            dst_ref=outs[index].at[:, mine, :],
            send_sem=o_send.at[index, 0],
            recv_sem=o_recv.at[index],
            device_id=at(0, 0, 1 - c),
            device_id_type=MESH,
        ).start()
        pltpu.make_async_copy(stage.at[index, :, :, lanes], outs[index].at[:, mine, :], o_send.at[index, 1]).start()

    give(0)
    give(1)

    arrived(PHI)

    def spread(z, _):
        in_z = layer_in(z, 4)
        halo_mask = halo_inside * in_z
        for t in range(TILES):
            u_a[z, t, own, :] = land[PHI][z, pl.ds(0, OWN), pl.ds(128 * t, 128)] * in_z
            halo = land[PHI][z, pl.ds(OWN, 8), pl.ds(128 * t, 128)] * halo_mask
            u_a[z, t, pl.ds(0, 8), :] = halo
            u_a[z, t, pl.ds(FIRST + OWN, 8), :] = halo
        return 0

    lax.fori_loop(0, NZ + 8, spread, 0, unroll=2)

    def sweep(src, dst, below, start, stop, charge=None):
        def body(z, _):
            _, sums = around(src, z, TOP, NR)
            weight = inside * (layer_in(z, below) * (1.0 / 6.0))
            for t in range(TILES):
                value = sums[t] * weight
                if charge is not None:
                    value = value + charge[z, t, pl.ds(TOP, NR), :]
                dst[z, t, pl.ds(TOP, NR), :] = value
            return 0

        lax.fori_loop(start, stop, body, 0, unroll=2)

    sweep(u_a, u_b, 4, 1, NZ + 7)
    sweep(u_b, u_a, 4, 2, NZ + 6)
    sweep(u_a, u_b, 4, 3, NZ + 5)

    def sweep_four(z, _):
        _, sums = around(u_b, z + 4, FIRST, OWN)
        for t in range(TILES):
            u_a[z, t, own, :] = sums[t] * (1.0 / 6.0)
        return 0

    lax.fori_loop(0, NZ, sweep_four, 0, unroll=2)

    for copy in copies:
        copy.wait_recv()

    @pl.when(lo_end)
    def _():
        for z in range(3):
            c_buf[z] = jnp.zeros((TILES, ROWS, 128), jnp.float32)

    @pl.when(hi_end)
    def _():
        for z in range(3 + NZ, 6 + NZ):
            c_buf[z] = jnp.zeros((TILES, ROWS, 128), jnp.float32)

    @pl.when(out_left)
    def _():
        for z in range(NZ + 6):
            c_buf[z, :, pl.ds(TOP, OFF), :] = jnp.zeros((TILES, OFF, 128), jnp.float32)

    @pl.when(out_right)
    def _():
        for z in range(NZ + 6):
            c_buf[z, :, pl.ds(FIRST + OWN, OFF), :] = jnp.zeros((TILES, OFF, 128), jnp.float32)

    sweep(c_buf, v_a, 3, 1, NZ + 5, c_buf)
    sweep(v_a, v_b, 3, 2, NZ + 4, c_buf)

    def last_sweep(z, _):
        _, sums = around(v_b, z + 3, FIRST, OWN)
        for t in range(TILES):
            stage[2, z, :, pl.ds(128 * t, 128)] = (sums[t] * (1.0 / 6.0) + c_buf[z + 3, t, own, :]) + u_a[z, t, own, :]
        return 0

    lax.fori_loop(0, NZ, last_sweep, 0, unroll=2)
    give(2)

    for copy in copies:
        copy.wait_send()
    for field in REACH:
        for dz in (-1, 0, 1):
            rows = sent_rows(field, dz)
            if rows:
                view = count.at[pl.ds(0, TILES // 2 * rows), :]
                pltpu.make_async_copy(view, view, in_send.at[field, dz + 1]).wait()
    for index in range(3):
        view = stage.at[index, :, :, pl.ds(0, NL)]
        for sem in (o_send.at[index, 0], o_send.at[index, 1], o_recv.at[index]):
            pltpu.make_async_copy(view, view, sem).wait()


def on_device(sizes, *fields):
    most = max(2 * max(received_rows(field), sent_rows(field, -1), sent_rows(field, 1)) for field in REACH)
    most = 2 * max(most, max(sent_rows(field, 0) for field in REACH))
    landing = [
        pltpu.VMEM(
            (NR, 2 * NL) if field in FLAT else (NZ + below + above, NR if rows else OWN, 2 * NL), fields[field].dtype
        )
        for field, (rows, below, above) in REACH.items()
    ]

    def work(*shape):
        return pltpu.VMEM(shape + (TILES, ROWS, 128), jnp.float32)

    dma = pltpu.SemaphoreType.DMA
    return pl.pallas_call(
        lambda *refs: kernel(sizes, *refs),
        out_shape=[jax.ShapeDtypeStruct((NZ, NR, NL), jnp.float32)] * 3,
        in_specs=[pl.BlockSpec(memory_space=pl.ANY)] * 8,
        out_specs=[pl.BlockSpec(memory_space=pl.ANY)] * 3,
        scratch_shapes=landing
        + [
            work(2, NZ + 4),
            pltpu.VMEM((2, NZ + 4, TILES, OWN, 128), jnp.float32),
            work(2, NZ + 4),
            work(2, NZ + 4),
            work(2, NZ + 4),
            work(NZ + 6),
            work(NZ + 6),
            work(NZ + 6),
            work(NZ + 8),
            work(NZ + 8),
            pltpu.VMEM((3, NZ, OWN, 2 * NL), jnp.float32),
            pltpu.VMEM((most, 128), jnp.float32),
            dma((8, 3)),
            dma((8,)),
            dma((8,)),
            dma((8,)),
            dma((3, 2)),
            dma((3,)),
        ],
        compiler_params=pltpu.CompilerParams(collective_id=0, has_side_effects=True, vmem_limit_bytes=48 << 20),
    )(*fields)


def solution(mesh):
    sizes = (mesh.shape["gz"], mesh.shape["gx"])
    in_specs = (P("gz", "gx", "gy"),) * 6 + (P("gx", "gy"),) * 2
    out_specs = (P("gz", "gx", "gy"),) * 3

    def step(
        electron_density, hole_density, potential, doping, electron_mobility, hole_mobility, cfl_map, fraction
    ):
        return tuple(
            on_device(
                sizes, electron_density, hole_density, electron_mobility, hole_mobility, potential, doping, cfl_map,
                fraction,
            )
        )

    return jax.shard_map(step, mesh=mesh, in_specs=in_specs, out_specs=out_specs, check_vma=False)
```

```python
import jax
import jax.numpy as jnp
from jax import lax
from jax.experimental import pallas as pl
from jax.experimental.pallas import tpu as pltpu
from jax.sharding import PartitionSpec as P

MESH = pl.DeviceIdType.MESH

CFL_MAX = 8
NZ = 16
NX = 16
NL = 256
OWN = 8
TILES = 4
ROWS = 32
FIRST = 8
LANDING = 24
TOP, SPAN = 4, 24
CHARGE = 3
SWEEPS = 4
DIFFUSION = 2
UP = CFL_MAX + 1 + DIFFUSION
LAYERS = OWN + 2 * DIFFUSION
SEAM = 8

E, H, ME, MH, PHI, DOP, CFL, FRAC = range(8)
REACH = {
    E: (DIFFUSION, UP, DIFFUSION),
    H: (DIFFUSION, DIFFUSION, UP),
    ME: (DIFFUSION, DIFFUSION, DIFFUSION),
    MH: (DIFFUSION, DIFFUSION, DIFFUSION),
    PHI: (SWEEPS, SWEEPS, SWEEPS),
    DOP: (0, 0, 0),
    CFL: (DIFFUSION, 0, 0),
    FRAC: (DIFFUSION, 0, 0),
}
FLAT = (CFL, FRAC)
GROUPS = ((ME, MH), (E, H, CFL, FRAC), (DOP,), (PHI,))
MOBILITIES, DENSITIES, DOPING, POTENTIAL = range(4)
SIDES = [(dz, dx) for dz in (1, -1, 0) for dx in (1, -1, 0)]


def piece(field, core, dz, dx):
    rows, below, above = REACH[field]
    if field in FLAT:
        along_z = (0, 0, 1 if dz == 0 else 0)
    else:
        start, stop = OWN * core - below, OWN * core + OWN + above
        if dz == 0:
            along_z = (max(start, 0), max(-start, 0), min(stop, NZ) - max(start, 0))
        elif dz == 1:
            along_z = (NZ + start, 0, -start)
        else:
            along_z = (0, NZ - start, stop - NZ)
    along_x = {0: (0, 0, NX), 1: (NX - rows, LANDING - rows, rows), -1: (0, NX, rows)}[dx]
    return (along_z, along_x) if along_z[2] > 0 and along_x[2] > 0 else None


def received(group, core, side):
    pieces = [piece(field, core, *side) for field in GROUPS[group]]
    return sum(TILES * p[0][2] * p[1][2] for p in pieces if p is not None)


def sent(side):
    total = 0
    for field in REACH:
        for core in (0, 1):
            p = piece(field, core, *side)
            if p is not None:
                total += TILES // 2 * p[0][2] * p[1][2]
    return total // 2 if side == (0, 0) else total


def kernel(sizes, *refs):
    n_gz, n_gx = sizes
    ins, outs, land = refs[:8], refs[8:11], refs[11:19]
    (s_buf, rs_buf, a_buf, q0, q1, result, c_buf, v_a, v_b, u_a, u_b, count, late, in_send, in_recv, c_send, c_recv, o_send,
     o_recv) = refs[19:]
    g, w, c = lax.axis_index("gz"), lax.axis_index("gx"), lax.axis_index("gy")
    lowest, highest, leftmost, rightmost = g == 0, g == n_gz - 1, w == 0, w == n_gx - 1

    def at(dz, dx, core):
        return (g + dz, w + dx, core)

    def both(*conditions):
        result = None
        for condition in conditions:
            if condition is not None:
                result = condition if result is None else jnp.logical_and(result, condition)
        return result

    def exists(dz, dx):
        return both(
            {1: jnp.logical_not(highest), -1: jnp.logical_not(lowest), 0: None}[dz],
            {1: jnp.logical_not(rightmost), -1: jnp.logical_not(leftmost), 0: None}[dx],
        )

    def when(condition, body):
        if condition is None:
            body()
        else:
            pl.when(condition)(body)

    seam_left = jnp.logical_and(lax.rem(w, SEAM) == 0, jnp.logical_not(leftmost))
    seam_right = jnp.logical_and(lax.rem(w, SEAM) == SEAM - 1, jnp.logical_not(rightmost))
    barrier = pltpu.get_barrier_semaphore()

    def greet(semaphore, dz, dx):
        if (dz, dx) == (0, 0):
            pl.semaphore_signal(semaphore, inc=1, device_id=at(0, 0, 1 - c), device_id_type=MESH)
        else:
            for core in (0, 1):
                pl.semaphore_signal(semaphore, inc=1, device_id=at(dz, dx, core), device_id_type=MESH)

    for dz, dx in SIDES:
        open_side = jnp.logical_not(seam_right) if dx == 1 else None
        when(both(exists(dz, dx), open_side), lambda dz=dz, dx=dx: greet(barrier, dz, dx))
    deep = 3 - lowest.astype(jnp.int32) - highest.astype(jnp.int32)
    wide = 3 - jnp.logical_or(leftmost, seam_left).astype(jnp.int32) - rightmost.astype(jnp.int32)
    pl.semaphore_wait(barrier, 2 * deep * wide - 1)
    for dz in (1, -1, 0):
        when(both(exists(dz, 1), seam_right), lambda dz=dz: greet(late, dz, 1))

    lanes = pl.ds(pl.multiple_of(c * NL, NL), NL)

    def push(group, side):
        dz, dx = side
        for field in GROUPS[group]:
            for core in (0, 1):
                p = piece(field, core, dz, dx)
                if p is None:
                    continue
                (src_z, dst_z, depth), (src_x, dst_x, rows) = p
                if field in FLAT:
                    src = ins[field].at[pl.ds(src_x, rows), :]
                    dst = land[field].at[pl.ds(dst_x, rows), lanes]
                else:
                    src = ins[field].at[pl.ds(src_z, depth), pl.ds(src_x, rows), :]
                    dst = land[field].at[pl.ds(dst_z, depth), pl.ds(dst_x, rows), lanes]
                sem = in_recv.at[group, 3 * dz + dx + 4]

                def remote(src=src, dst=dst, sem=sem, core=core):
                    pltpu.make_async_remote_copy(
                        src_ref=src,
                        dst_ref=dst,
                        send_sem=in_send.at[3 * dz + dx + 4],
                        recv_sem=sem,
                        device_id=at(dz, dx, core),
                        device_id_type=MESH,
                    ).start()

                def local(src=src, dst=dst, sem=sem):
                    pltpu.make_async_copy(src, dst, sem).start()

                if side == (0, 0):
                    pl.when(c == core)(local)
                    pl.when(c != core)(remote)
                else:
                    remote()

    def push_all(group, sides, condition=None):
        for side in sides:
            when(both(exists(*side), condition), lambda side=side: push(group, side))

    def wait_rows(rows, sem):
        view = count.at[pl.ds(0, rows), :]
        pltpu.make_async_copy(view, view, sem).wait()

    def arrived(group):
        for dz, dx in SIDES:
            for core in (0, 1):
                rows = received(group, core, (dz, dx))
                if rows == 0:
                    continue
                even = core == 1 or received(group, 1, (dz, dx)) != rows
                if core == 1 and received(group, 0, (dz, dx)) == rows:
                    continue
                mine = c == core if even else None
                sem = in_recv.at[group, 3 * dz + dx + 4]
                when(both(exists(-dz, -dx), mine), lambda rows=rows, sem=sem: wait_rows(rows, sem))

    right = [(dz, 1) for dz in (1, -1, 0)]
    left = [(dz, -1) for dz in (1, -1, 0)]
    near = [(1, 0), (-1, 0), (0, 0)]
    for group in range(4):
        push_all(group, right)
        push_all(group, left, jnp.logical_not(seam_left))
        push_all(group, near)

    @pl.when(seam_left)
    def _():
        pl.semaphore_wait(late, 2 * deep)
        for group in range(4):
            push_all(group, left)

    def splat(flag, rows):
        return jnp.broadcast_to(flag.astype(jnp.int32), (rows, 128)) > 0

    has_left, has_right = jnp.logical_not(leftmost), jnp.logical_not(rightmost)
    row = lax.broadcasted_iota(jnp.int32, (SPAN, 128), 0) + (TOP - FIRST)
    first_row = jnp.where(leftmost, 0, -FIRST)
    last_row = jnp.where(rightmost, NX, NX + FIRST)
    inside = jnp.logical_and(row >= first_row, row < last_row)
    sixth = jnp.where(inside, 1.0 / 6.0, 0.0)
    halo_row = lax.broadcasted_iota(jnp.int32, (8, 128), 0)
    halo_inside = jnp.where(halo_row < 4, has_right.astype(jnp.int32), has_left.astype(jnp.int32))
    lane = lax.broadcasted_iota(jnp.int32, (SPAN, 128), 1)
    at_first, at_last = lane == 0, lane == 127

    def layer_in(z, below):
        z = z - below + OWN * c
        return jnp.logical_and(jnp.logical_or(z >= 0, jnp.logical_not(lowest)), jnp.logical_or(z < NZ, jnp.logical_not(highest)))

    def around(ref, z, start, rows):
        centre = [ref[z, t, pl.ds(start, rows), :] for t in range(TILES)]
        up = [pltpu.roll(v, 127, 1) for v in centre] + [jnp.zeros((rows, 128), jnp.float32)]
        down = [jnp.zeros((rows, 128), jnp.float32)] + [pltpu.roll(v, 1, 1) for v in centre]
        is_first, is_last = at_first[:rows], at_last[:rows]
        sums = []
        for t in range(TILES):
            in_y = jnp.where(is_last, up[t + 1], up[t]) + jnp.where(is_first, down[t], down[t + 1])
            in_z = ref[z + 1, t, pl.ds(start, rows), :] + ref[z - 1, t, pl.ds(start, rows), :]
            in_x = ref[z, t, pl.ds(start + 1, rows), :] + ref[z, t, pl.ds(start - 1, rows), :]
            sums.append((in_z + in_x) + in_y)
        return centre, sums

    def empty(field, start, layers):
        for z in range(start, start + layers):
            land[field][z] = jnp.zeros((LANDING, 2 * NL), jnp.float32)

    for core in (0, 1):

        @pl.when(jnp.logical_and(lowest, c == core))
        def _(core=core):
            empty(E, 0, UP - OWN * core)
            if core == 0:
                empty(H, 0, DIFFUSION)

        @pl.when(jnp.logical_and(highest, c == core))
        def _(core=core):
            empty(H, DIFFUSION + NZ - OWN * core, UP - OWN * (1 - core))
            if core == 1:
                empty(E, UP + OWN, DIFFUSION)

    arrived(MOBILITIES)
    own, halo = pl.ds(FIRST, NX), pl.ds(NX, 8)
    after, before = pl.ds(FIRST + NX, 8), pl.ds(0, 8)

    def roots(z, _):
        in_z = layer_in(z, DIFFUSION).astype(jnp.int32)
        own_mask, halo_mask = jnp.broadcast_to(in_z, (NX, 128)) > 0, halo_inside * in_z > 0
        for kind, field in ((0, ME), (1, MH)):
            for t in range(TILES):
                m = land[field][z, pl.ds(0, NX), pl.ds(128 * t, 128)]
                rs = lax.rsqrt(m)
                rs_buf[kind, z, t] = rs
                s_buf[kind, z, t, own, :] = jnp.where(own_mask, m * rs, 0.0)
                m = land[field][z, halo, pl.ds(128 * t, 128)]
                s = jnp.where(halo_mask, m * lax.rsqrt(m), 0.0)
                s_buf[kind, z, t, before, :] = s
                s_buf[kind, z, t, after, :] = s
        return 0

    lax.fori_loop(0, LAYERS, roots, 0)

    def stays(z, _):
        for kind in (0, 1):
            centre, sums = around(s_buf.at[kind], z, TOP, SPAN)
            for t in range(TILES):
                a_buf[kind, z, t, pl.ds(TOP, SPAN), :] = 1.0 - centre[t] * sums[t]
        return 0

    lax.fori_loop(1, LAYERS - 1, stays, 0)

    arrived(DENSITIES)
    for from_row, to_row in ((0, 8), (8, 16), (16, 24)):
        rows, target = pl.ds(from_row, 8), pl.ds(to_row, 8)

        def drift(t, _, rows=rows, target=target, at_halo=from_row == NX):
            tile = pl.ds(pl.multiple_of(t * 128, 128), 128)
            d = land[CFL][rows, tile]
            f = land[FRAC][rows, tile]
            rest = 1.0 - f
            bits = [(k, jnp.bitwise_and(d, k) != 0) for k in (8, 4, 2, 1)]
            mask = halo_inside > 0
            for kind, field in ((0, E), (1, H)):
                length = LAYERS + CFL_MAX + 1
                if kind == 0:
                    v = [land[field][length - 1 - i, rows, tile] for i in range(length)]
                else:
                    v = [land[field][i, rows, tile] for i in range(length)]
                for k, bit in bits:
                    if k == 8:
                        v = [jnp.where(bit, v[i + 8], v[i]) if i <= LAYERS else v[i] for i in range(length - 1)]
                    else:
                        v = [jnp.where(bit, v[i + k], v[i]) for i in range(len(v) - k)]
                for i in range(LAYERS):
                    z = LAYERS - 1 - i if kind == 0 else i
                    q = (rest * v[i] + f * v[i + 1]) * s_buf[kind, z, t, target, :]
                    if at_halo:
                        q = jnp.where(mask, q, 0.0)
                        q0[kind, z, t, before, :] = q
                    q0[kind, z, t, target, :] = q
            return 0

        lax.fori_loop(0, TILES, drift, 0)

    span = pl.ds(TOP, SPAN)

    def sweep_one(z, _):
        for kind in (0, 1):
            centre, sums = around(q0.at[kind], z, TOP, SPAN)
            for t in range(TILES):
                s = s_buf[kind, z, t, span, :]
                q1[kind, z, t, span, :] = centre[t] * a_buf[kind, z, t, span, :] + (s * s) * sums[t]
        return 0

    lax.fori_loop(1, LAYERS - 1, sweep_one, 0)

    arrived(DOPING)

    def sweep_two(z, _):
        found = []
        for kind in (0, 1):
            centre, sums = around(q1.at[kind], z + DIFFUSION, FIRST, NX)
            n = []
            for t in range(TILES):
                s = s_buf[kind, z + DIFFUSION, t, own, :]
                q = centre[t] * a_buf[kind, z + DIFFUSION, t, own, :] + (s * s) * sums[t]
                n.append(q * rs_buf[kind, z + DIFFUSION, t])
                result[kind, z, t, own, :] = n[t]
            found.append(n)
        for t in range(TILES):
            doping = land[DOP][z, pl.ds(0, NX), pl.ds(128 * t, 128)]
            c_buf[z + CHARGE, t, own, :] = (found[1][t] - found[0][t] + doping) * (0.5 / 6.0)
        return 0

    lax.fori_loop(0, OWN, sweep_two, 0)

    above_there, below_there = jnp.logical_or(c == 0, jnp.logical_not(highest)), jnp.logical_or(c == 1, jnp.logical_not(lowest))
    upward, downward = c, c - 1

    def exchange(ways, start):
        for dz, dx in ways:
            depth, rows = (CHARGE, NX) if dx == 0 else (CHARGE - 1, CHARGE - 1) if dz != 0 else (OWN, CHARGE)
            src_z, dst_z = {1: (CHARGE + OWN - depth, CHARGE - depth), -1: (CHARGE, CHARGE + OWN), 0: (CHARGE, CHARGE)}[dz]
            src_x, dst_x = {1: (FIRST + NX - rows, FIRST - rows), -1: (FIRST, FIRST + NX), 0: (FIRST, FIRST)}[dx]
            way = 3 * dz + dx + 4
            chip = {1: upward, -1: downward, 0: 0}[dz]
            core = c if dz == 0 else 1 - c

            def one(src_z=src_z, dst_z=dst_z, src_x=src_x, dst_x=dst_x, depth=depth, rows=rows, way=way, chip=chip, core=core, dx=dx):
                copy = pltpu.make_async_remote_copy(
                    src_ref=c_buf.at[pl.ds(src_z, depth), :, pl.ds(src_x, rows), :],
                    dst_ref=c_buf.at[pl.ds(dst_z, depth), :, pl.ds(dst_x, rows), :],
                    send_sem=c_send.at[way],
                    recv_sem=c_recv.at[way],
                    device_id=at(chip, dx, core),
                    device_id_type=MESH,
                )
                if start:
                    copy.start()
                else:
                    copy.wait_send()

            when(both({1: above_there, -1: below_there, 0: None}[dz], exists(0, dx)), one)

    def charge_arrived(ways):
        for dz, dx in ways:
            depth, rows = (CHARGE, NX) if dx == 0 else (CHARGE - 1, CHARGE - 1) if dz != 0 else (OWN, CHARGE)
            view = c_buf.at[pl.ds(0, depth), :, pl.ds(0, rows), :]
            way = 3 * dz + dx + 4

            def one(view=view, way=way):
                pltpu.make_async_copy(view, view, c_recv.at[way]).wait()

            when(both({1: below_there, -1: above_there, 0: None}[dz], exists(0, -dx)), one)

    ways = [(1, 1), (-1, 1), (1, -1), (-1, -1), (0, 1), (0, -1), (1, 0), (-1, 0)]
    exchange(ways, True)

    mine = pl.ds(pl.multiple_of(c * OWN, OWN), OWN)

    def give(index):
        for k in range(TILES // 2):
            there = outs[index].at[mine, :, pl.ds(128 * k, 128)]
            pltpu.make_async_remote_copy(
                src_ref=result.at[index, :, 2 * (1 - c) + k, pl.ds(FIRST, NX), :],
                dst_ref=there,
                send_sem=o_send.at[index, k],
                recv_sem=o_recv.at[index, k],
                device_id=at(0, 0, 1 - c),
                device_id_type=MESH,
            ).start()
            pltpu.make_async_copy(result.at[index, :, 2 * c + k, pl.ds(FIRST, NX), :], there, o_send.at[index, 2 + k]).start()

    give(0)
    give(1)

    arrived(POTENTIAL)

    def spread(z, _):
        in_z = layer_in(z, SWEEPS).astype(jnp.int32)
        own_mask, halo_mask = jnp.broadcast_to(in_z, (NX, 128)) > 0, halo_inside * in_z > 0
        for t in range(TILES):
            tile = pl.ds(128 * t, 128)
            u_a[z, t, own, :] = jnp.where(own_mask, land[PHI][z, pl.ds(0, NX), tile], 0.0)
            phi = jnp.where(halo_mask, land[PHI][z, halo, tile], 0.0)
            u_a[z, t, before, :] = phi
            u_a[z, t, after, :] = phi
        return 0

    lax.fori_loop(0, OWN + 2 * SWEEPS, spread, 0)

    def sweep(src, dst, below, start, stop, charge=None):
        def body(z, _):
            _, sums = around(src, z, TOP, SPAN)
            weight = jnp.where(splat(layer_in(z, below), SPAN), sixth, 0.0)
            for t in range(TILES):
                value = sums[t] * weight
                if charge is not None:
                    value = value + charge[z, t, span, :]
                dst[z, t, span, :] = value
            return 0

        lax.fori_loop(start, stop, body, 0, unroll=2)

    sweep(u_a, u_b, SWEEPS, 1, OWN + 2 * SWEEPS - 1)
    sweep(u_b, u_a, SWEEPS, 2, OWN + 2 * SWEEPS - 2)
    sweep(u_a, u_b, SWEEPS, 3, OWN + 2 * SWEEPS - 3)

    def sweep_four(z, _):
        _, sums = around(u_b, z + SWEEPS, FIRST, NX)
        for t in range(TILES):
            u_a[z, t, own, :] = sums[t] * (1.0 / 6.0)
        return 0

    lax.fori_loop(0, OWN, sweep_four, 0, unroll=2)

    def clear(condition, start, layers, first, rows):
        @pl.when(condition)
        def _():
            for z in range(start, start + layers):
                c_buf[z, :, pl.ds(first, rows), :] = jnp.zeros((TILES, rows, 128), jnp.float32)

    clear(jnp.logical_not(below_there), 0, CHARGE, 0, ROWS)
    clear(jnp.logical_not(above_there), CHARGE + OWN, CHARGE, 0, ROWS)
    clear(leftmost, 0, OWN + 2 * CHARGE, TOP, FIRST - TOP)
    clear(rightmost, 0, OWN + 2 * CHARGE, FIRST + NX, FIRST - TOP)
    charge_arrived(ways)

    sweep(c_buf, v_a, CHARGE, 1, OWN + 2 * CHARGE - 1, c_buf)
    sweep(v_a, v_b, CHARGE, 2, OWN + 2 * CHARGE - 2, c_buf)

    def last_sweep(z, _):
        _, sums = around(v_b, z + CHARGE, FIRST, NX)
        for t in range(TILES):
            result[2, z, t, own, :] = (sums[t] * (1.0 / 6.0) + c_buf[z + CHARGE, t, own, :]) + u_a[z, t, own, :]
        return 0

    lax.fori_loop(0, OWN, last_sweep, 0, unroll=2)
    give(2)

    exchange(ways, False)
    for dz, dx in SIDES:
        when(exists(dz, dx), lambda dz=dz, dx=dx: wait_rows(sent((dz, dx)), in_send.at[3 * dz + dx + 4]))
    for index in range(3):
        view = result.at[index, :, 0, own, :]
        for k in range(TILES // 2):
            for sem in (o_send.at[index, k], o_send.at[index, 2 + k], o_recv.at[index, k]):
                pltpu.make_async_copy(view, view, sem).wait()


def hand_over(*refs):
    ins, outs, sems = refs[:3], refs[3:6], refs[6]
    copies = [pltpu.make_async_copy(ins[k], outs[k], sems.at[k]) for k in range(3)]
    for copy in copies:
        copy.start()
    for copy in copies:
        copy.wait()


def on_device(sizes, *fields):
    most = max(max(sent(side), received(group, core, side)) for side in SIDES for group in range(4) for core in (0, 1))
    landing = [
        pltpu.VMEM(
            (LANDING, 2 * NL) if field in FLAT else (OWN + below + above, LANDING if rows else NX, 2 * NL), fields[field].dtype
        )
        for field, (rows, below, above) in REACH.items()
    ]

    def work(*shape):
        return pltpu.VMEM(shape + (TILES, ROWS, 128), jnp.float32)

    dma = pltpu.SemaphoreType.DMA
    shapes = [jax.ShapeDtypeStruct((NZ, NX, NL), jnp.float32)] * 3
    found = pl.pallas_call(
        lambda *refs: kernel(sizes, *refs),
        out_shape=[pltpu.VMEM((NZ, NX, NL), jnp.float32)] * 3,
        in_specs=[pl.BlockSpec(memory_space=pl.ANY)] * 8,
        out_specs=[pl.BlockSpec(memory_space=pl.ANY)] * 3,
        scratch_shapes=landing
        + [
            work(2, LAYERS),
            pltpu.VMEM((2, LAYERS, TILES, NX, 128), jnp.float32),
            work(2, LAYERS),
            work(2, LAYERS),
            work(2, LAYERS),
            work(3, OWN),
            work(OWN + 2 * CHARGE),
            work(OWN + 2 * CHARGE),
            work(OWN + 2 * CHARGE),
            work(OWN + 2 * SWEEPS),
            work(OWN + 2 * SWEEPS),
            pltpu.VMEM((most, 128), jnp.float32),
            pltpu.SemaphoreType.REGULAR,
            dma((9,)),
            dma((4, 9)),
            dma((9,)),
            dma((9,)),
            dma((3, 4)),
            dma((3, 2)),
        ],
        compiler_params=pltpu.CompilerParams(collective_id=0, has_side_effects=True, vmem_limit_bytes=60 << 20),
    )(*fields)
    return pl.pallas_call(
        hand_over,
        out_shape=shapes,
        in_specs=[pl.BlockSpec(memory_space=pl.ANY)] * 3,
        out_specs=[pl.BlockSpec(memory_space=pl.ANY)] * 3,
        scratch_shapes=[dma((3,))],
        compiler_params=pltpu.CompilerParams(vmem_limit_bytes=8 << 20),
    )(*found)


def solution(mesh):
    sizes = (mesh.shape["gz"], mesh.shape["gx"])
    in_specs = (P("gz", "gx", "gy"),) * 6 + (P("gx", "gy"),) * 2
    out_specs = (P("gz", "gx", "gy"),) * 3

    def step(
        electron_density, hole_density, potential, doping, electron_mobility, hole_mobility, cfl_map, fraction
    ):
        return tuple(
            on_device(
                sizes, electron_density, hole_density, electron_mobility, hole_mobility, potential, doping, cfl_map,
                fraction,
            )
        )

    return jax.shard_map(step, mesh=mesh, in_specs=in_specs, out_specs=out_specs, check_vma=False)
```

```python
import jax
import jax.numpy as jnp
from jax import lax
from jax.experimental import pallas as pl
from jax.experimental.pallas import tpu as pltpu
from jax.sharding import PartitionSpec as P

MESH = pl.DeviceIdType.MESH

CFL_MAX = 8
NZ = 16
NX = 16
NL = 256
OWN = 8
TILES = 4
ROWS = 32
FIRST = 8
LANDING = 24
TOP, SPAN = 4, 24
CHARGE = 3
EARLY = 2
DIFFUSION = 2
UP = CFL_MAX + 1 + DIFFUSION
LAYERS = OWN + 2 * DIFFUSION
SEAM = 8

E, H, ME, MH, PHI, DOP, CFL, FRAC = range(8)
REACH = {
    E: (DIFFUSION, UP, DIFFUSION),
    H: (DIFFUSION, DIFFUSION, UP),
    ME: (DIFFUSION, DIFFUSION, DIFFUSION),
    MH: (DIFFUSION, DIFFUSION, DIFFUSION),
    PHI: (EARLY, EARLY, EARLY),
    DOP: (0, 0, 0),
    CFL: (DIFFUSION, 0, 0),
    FRAC: (DIFFUSION, 0, 0),
}
FLAT = (CFL, FRAC)
GROUPS = ((ME, MH), (PHI,), (E, H, CFL, FRAC), (DOP,))
MOBILITIES, POTENTIAL, DENSITIES, DOPING = range(4)
SIDES = [(dz, dx) for dz in (1, -1, 0) for dx in (1, -1, 0)]


def piece(field, core, dz, dx):
    rows, below, above = REACH[field]
    if field in FLAT:
        along_z = (0, 0, 1 if dz == 0 else 0)
    else:
        base = OWN * core - below
        start, stop = base + abs(dx), OWN * core + OWN + above - abs(dx)
        if dz == 0:
            start, stop = max(start, 0), min(stop, NZ)
            along_z = (start, start - base, stop - start)
        elif dz == 1:
            along_z = (NZ + start, start - base, -start)
        else:
            along_z = (0, NZ - base, stop - NZ)
    along_x = {0: (0, 0, NX), 1: (NX - rows, LANDING - rows, rows), -1: (0, NX, rows)}[dx]
    return (along_z, along_x) if along_z[2] > 0 and along_x[2] > 0 else None


def received(group, core, side):
    pieces = [piece(field, core, *side) for field in GROUPS[group]]
    return sum(TILES * p[0][2] * p[1][2] for p in pieces if p is not None)


def sent(side):
    total = 0
    for field in REACH:
        for core in (0, 1):
            p = piece(field, core, *side)
            if p is not None:
                total += TILES // 2 * p[0][2] * p[1][2]
    return total // 2 if side == (0, 0) else total


def kernel(sizes, *refs):
    n_gz, n_gx = sizes
    ins, outs, land = refs[:8], refs[8:11], refs[11:19]
    (s_buf, rs_buf, a_buf, q0, q1, result, c_buf, u2, v_a, v_b, u_a, u_b, count, late, in_send, in_recv, c_send, c_recv,
     o_send, o_recv) = refs[19:]
    g, w, c = lax.axis_index("gz"), lax.axis_index("gx"), lax.axis_index("gy")
    lowest, highest, leftmost, rightmost = g == 0, g == n_gz - 1, w == 0, w == n_gx - 1

    def at(dz, dx, core):
        return (g + dz, w + dx, core)

    def both(*conditions):
        result = None
        for condition in conditions:
            if condition is not None:
                result = condition if result is None else jnp.logical_and(result, condition)
        return result

    def exists(dz, dx):
        return both(
            {1: jnp.logical_not(highest), -1: jnp.logical_not(lowest), 0: None}[dz],
            {1: jnp.logical_not(rightmost), -1: jnp.logical_not(leftmost), 0: None}[dx],
        )

    def when(condition, body):
        if condition is None:
            body()
        else:
            pl.when(condition)(body)

    seam_left = jnp.logical_and(lax.rem(w, SEAM) == 0, jnp.logical_not(leftmost))
    seam_right = jnp.logical_and(lax.rem(w, SEAM) == SEAM - 1, jnp.logical_not(rightmost))
    barrier = pltpu.get_barrier_semaphore()

    def greet(semaphore, dz, dx):
        if (dz, dx) == (0, 0):
            pl.semaphore_signal(semaphore, inc=1, device_id=at(0, 0, 1 - c), device_id_type=MESH)
        else:
            for core in (0, 1):
                pl.semaphore_signal(semaphore, inc=1, device_id=at(dz, dx, core), device_id_type=MESH)

    for dz, dx in SIDES:
        open_side = jnp.logical_not(seam_right) if dx == 1 else None
        when(both(exists(dz, dx), open_side), lambda dz=dz, dx=dx: greet(barrier, dz, dx))
    deep = 3 - lowest.astype(jnp.int32) - highest.astype(jnp.int32)
    wide = 3 - jnp.logical_or(leftmost, seam_left).astype(jnp.int32) - rightmost.astype(jnp.int32)
    pl.semaphore_wait(barrier, 2 * deep * wide - 1)
    for dz in (1, -1, 0):
        when(both(exists(dz, 1), seam_right), lambda dz=dz: greet(late, dz, 1))

    lanes = pl.ds(pl.multiple_of(c * NL, NL), NL)

    def push(group, side):
        dz, dx = side
        for field in GROUPS[group]:
            for core in (0, 1):
                p = piece(field, core, dz, dx)
                if p is None:
                    continue
                (src_z, dst_z, depth), (src_x, dst_x, rows) = p
                if field in FLAT:
                    src = ins[field].at[pl.ds(src_x, rows), :]
                    dst = land[field].at[pl.ds(dst_x, rows), lanes]
                else:
                    src = ins[field].at[pl.ds(src_z, depth), pl.ds(src_x, rows), :]
                    dst = land[field].at[pl.ds(dst_z, depth), pl.ds(dst_x, rows), lanes]
                sem = in_recv.at[group, 3 * dz + dx + 4]

                def remote(src=src, dst=dst, sem=sem, core=core):
                    pltpu.make_async_remote_copy(
                        src_ref=src,
                        dst_ref=dst,
                        send_sem=in_send.at[3 * dz + dx + 4],
                        recv_sem=sem,
                        device_id=at(dz, dx, core),
                        device_id_type=MESH,
                    ).start()

                def local(src=src, dst=dst, sem=sem):
                    pltpu.make_async_copy(src, dst, sem).start()

                if side == (0, 0):
                    pl.when(c == core)(local)
                    pl.when(c != core)(remote)
                else:
                    remote()

    def push_all(group, sides, condition=None):
        for side in sides:
            when(both(exists(*side), condition), lambda side=side: push(group, side))

    def wait_rows(rows, sem):
        view = count.at[pl.ds(0, rows), :]
        pltpu.make_async_copy(view, view, sem).wait()

    def arrived(group):
        for dz, dx in SIDES:
            for core in (0, 1):
                rows = received(group, core, (dz, dx))
                if rows == 0:
                    continue
                even = core == 1 or received(group, 1, (dz, dx)) != rows
                if core == 1 and received(group, 0, (dz, dx)) == rows:
                    continue
                mine = c == core if even else None
                sem = in_recv.at[group, 3 * dz + dx + 4]
                when(both(exists(-dz, -dx), mine), lambda rows=rows, sem=sem: wait_rows(rows, sem))

    right = [(dz, 1) for dz in (1, -1, 0)]
    left = [(dz, -1) for dz in (1, -1, 0)]
    near = [(1, 0), (-1, 0), (0, 0)]
    for group in range(4):
        push_all(group, right)
        push_all(group, left, jnp.logical_not(seam_left))
        push_all(group, near)

    @pl.when(seam_left)
    def _():
        pl.semaphore_wait(late, 2 * deep)
        for group in range(4):
            push_all(group, left)

    def splat(flag, rows):
        return jnp.broadcast_to(flag.astype(jnp.int32), (rows, 128)) > 0

    has_left, has_right = jnp.logical_not(leftmost), jnp.logical_not(rightmost)
    row = lax.broadcasted_iota(jnp.int32, (SPAN, 128), 0) + (TOP - FIRST)
    first_row = jnp.where(leftmost, 0, -FIRST)
    last_row = jnp.where(rightmost, NX, NX + FIRST)
    inside = jnp.logical_and(row >= first_row, row < last_row)
    sixth = jnp.where(inside, 1.0 / 6.0, 0.0)
    halo_row = lax.broadcasted_iota(jnp.int32, (8, 128), 0)
    halo_inside = jnp.where(halo_row < 4, has_right.astype(jnp.int32), has_left.astype(jnp.int32))
    lane = lax.broadcasted_iota(jnp.int32, (SPAN, 128), 1)
    at_first, at_last = lane == 0, lane == 127

    def layer_in(z, below):
        z = z - below + OWN * c
        return jnp.logical_and(jnp.logical_or(z >= 0, jnp.logical_not(lowest)), jnp.logical_or(z < NZ, jnp.logical_not(highest)))

    def around(ref, z, start, rows):
        centre = [ref[z, t, pl.ds(start, rows), :] for t in range(TILES)]
        up = [pltpu.roll(v, 127, 1) for v in centre] + [jnp.zeros((rows, 128), jnp.float32)]
        down = [jnp.zeros((rows, 128), jnp.float32)] + [pltpu.roll(v, 1, 1) for v in centre]
        is_first, is_last = at_first[:rows], at_last[:rows]
        sums = []
        for t in range(TILES):
            in_y = jnp.where(is_last, up[t + 1], up[t]) + jnp.where(is_first, down[t], down[t + 1])
            in_z = ref[z + 1, t, pl.ds(start, rows), :] + ref[z - 1, t, pl.ds(start, rows), :]
            in_x = ref[z, t, pl.ds(start + 1, rows), :] + ref[z, t, pl.ds(start - 1, rows), :]
            sums.append((in_z + in_x) + in_y)
        return centre, sums

    def empty(field, start, layers):
        for z in range(start, start + layers):
            land[field][z] = jnp.zeros((LANDING, 2 * NL), jnp.float32)

    for core in (0, 1):

        @pl.when(jnp.logical_and(lowest, c == core))
        def _(core=core):
            empty(E, 0, UP - OWN * core)
            if core == 0:
                empty(H, 0, DIFFUSION)

        @pl.when(jnp.logical_and(highest, c == core))
        def _(core=core):
            empty(H, DIFFUSION + NZ - OWN * core, UP - OWN * (1 - core))
            if core == 1:
                empty(E, UP + OWN, DIFFUSION)

    arrived(MOBILITIES)
    own, halo = pl.ds(FIRST, NX), pl.ds(NX, 8)
    after, before = pl.ds(FIRST + NX, 8), pl.ds(0, 8)

    def roots(z, _):
        in_z = layer_in(z, DIFFUSION).astype(jnp.int32)
        own_mask, halo_mask = jnp.broadcast_to(in_z, (NX, 128)) > 0, halo_inside * in_z > 0
        for kind, field in ((0, ME), (1, MH)):
            for t in range(TILES):
                m = land[field][z, pl.ds(0, NX), pl.ds(128 * t, 128)]
                rs = lax.rsqrt(m)
                rs_buf[kind, z, t] = rs
                s_buf[kind, z, t, own, :] = jnp.where(own_mask, m * rs, 0.0)
                m = land[field][z, halo, pl.ds(128 * t, 128)]
                s = jnp.where(halo_mask, m * lax.rsqrt(m), 0.0)
                s_buf[kind, z, t, before, :] = s
                s_buf[kind, z, t, after, :] = s
        return 0

    lax.fori_loop(0, LAYERS, roots, 0, unroll=2)

    def stays(z, _):
        for kind in (0, 1):
            centre, sums = around(s_buf.at[kind], z, TOP, SPAN)
            for t in range(TILES):
                a_buf[kind, z, t, pl.ds(TOP, SPAN), :] = 1.0 - centre[t] * sums[t]
        return 0

    lax.fori_loop(1, LAYERS - 1, stays, 0, unroll=5)

    above_there, below_there = jnp.logical_or(c == 0, jnp.logical_not(highest)), jnp.logical_or(c == 1, jnp.logical_not(lowest))
    upward, downward = c, c - 1

    def shape(deep, dz, dx):
        return (deep, NX) if dx == 0 else (deep - 1, deep - 1) if dz != 0 else (OWN, deep)

    def exchange(buf, k, deep, ways, start):
        for dz, dx in ways:
            depth, rows = shape(deep, dz, dx)
            src_z, dst_z = {1: (CHARGE + OWN - depth, CHARGE - depth), -1: (CHARGE, CHARGE + OWN), 0: (CHARGE, CHARGE)}[dz]
            src_x, dst_x = {1: (FIRST + NX - rows, FIRST - rows), -1: (FIRST, FIRST + NX), 0: (FIRST, FIRST)}[dx]
            way = 3 * dz + dx + 4
            chip = {1: upward, -1: downward, 0: 0}[dz]
            core = c if dz == 0 else 1 - c
            src = buf.at[pl.ds(src_z, depth), :, pl.ds(src_x, rows), :]
            dst = buf.at[pl.ds(dst_z, depth), :, pl.ds(dst_x, rows), :]

            def one(src=src, dst=dst, way=way, target=at(chip, dx, core)):
                copy = pltpu.make_async_remote_copy(
                    src_ref=src,
                    dst_ref=dst,
                    send_sem=c_send.at[k, way],
                    recv_sem=c_recv.at[k, way],
                    device_id=target,
                    device_id_type=MESH,
                )
                if start:
                    copy.start()
                else:
                    copy.wait_send()

            when(both({1: above_there, -1: below_there, 0: None}[dz], exists(0, dx)), one)

    def exchanged(buf, k, deep, ways):
        for dz, dx in ways:
            depth, rows = shape(deep, dz, dx)
            view = buf.at[pl.ds(0, depth), :, pl.ds(0, rows), :]
            way = 3 * dz + dx + 4

            def one(view=view, way=way):
                pltpu.make_async_copy(view, view, c_recv.at[k, way]).wait()

            when(both({1: below_there, -1: above_there, 0: None}[dz], exists(0, -dx)), one)

    def clear_outside(buf):
        def clear(condition, start, layers, first, rows):
            @pl.when(condition)
            def _():
                for z in range(start, start + layers):
                    buf[z, :, pl.ds(first, rows), :] = jnp.zeros((TILES, rows, 128), jnp.float32)

        clear(jnp.logical_not(below_there), 0, CHARGE, 0, ROWS)
        clear(jnp.logical_not(above_there), CHARGE + OWN, CHARGE, 0, ROWS)
        clear(leftmost, 0, OWN + 2 * CHARGE, TOP, FIRST - TOP)
        clear(rightmost, 0, OWN + 2 * CHARGE, FIRST + NX, FIRST - TOP)

    ways = [(1, 1), (-1, 1), (1, -1), (-1, -1), (0, 1), (0, -1), (1, 0), (-1, 0)]
    arrived(POTENTIAL)

    def spread(z, _):
        in_z = layer_in(z, EARLY).astype(jnp.int32)
        own_mask, halo_mask = jnp.broadcast_to(in_z, (NX, 128)) > 0, halo_inside * in_z > 0
        for t in range(TILES):
            tile = pl.ds(128 * t, 128)
            u_a[z, t, own, :] = jnp.where(own_mask, land[PHI][z, pl.ds(0, NX), tile], 0.0)
            phi = jnp.where(halo_mask, land[PHI][z, halo, tile], 0.0)
            u_a[z, t, before, :] = phi
            u_a[z, t, after, :] = phi
        return 0

    lax.fori_loop(0, OWN + 2 * EARLY, spread, 0, unroll=2)

    span = pl.ds(TOP, SPAN)

    def first_sweep(z, _):
        _, sums = around(u_a, z, TOP, SPAN)
        weight = jnp.where(splat(layer_in(z, EARLY), SPAN), sixth, 0.0)
        for t in range(TILES):
            u_b[z, t, span, :] = sums[t] * weight
        return 0

    lax.fori_loop(1, OWN + 2 * EARLY - 1, first_sweep, 0, unroll=5)

    def second_sweep(z, _):
        _, sums = around(u_b, z + EARLY, FIRST, NX)
        for t in range(TILES):
            u2[z + CHARGE, t, own, :] = sums[t] * (1.0 / 6.0)
        return 0

    lax.fori_loop(0, OWN, second_sweep, 0, unroll=4)
    exchange(u2, 1, EARLY, ways, True)
    clear_outside(u2)
    clear_outside(c_buf)

    arrived(DENSITIES)
    for from_row, to_row in ((0, 8), (8, 16), (16, 24)):
        rows, target = pl.ds(from_row, 8), pl.ds(to_row, 8)

        def drift(t, _, rows=rows, target=target, at_halo=from_row == NX):
            tile = pl.ds(pl.multiple_of(t * 128, 128), 128)
            d = land[CFL][rows, tile]
            f = land[FRAC][rows, tile]
            rest = 1.0 - f
            bits = [(k, jnp.bitwise_and(d, k) != 0) for k in (8, 4, 2, 1)]
            mask = halo_inside > 0
            for kind, field in ((0, E), (1, H)):
                length = LAYERS + CFL_MAX + 1
                if kind == 0:
                    v = [land[field][length - 1 - i, rows, tile] for i in range(length)]
                else:
                    v = [land[field][i, rows, tile] for i in range(length)]
                for k, bit in bits:
                    if k == 8:
                        v = [jnp.where(bit, v[i + 8], v[i]) if i <= LAYERS else v[i] for i in range(length - 1)]
                    else:
                        v = [jnp.where(bit, v[i + k], v[i]) for i in range(len(v) - k)]
                for i in range(LAYERS):
                    z = LAYERS - 1 - i if kind == 0 else i
                    q = (rest * v[i] + f * v[i + 1]) * s_buf[kind, z, t, target, :]
                    if at_halo:
                        q = jnp.where(mask, q, 0.0)
                        q0[kind, z, t, before, :] = q
                    q0[kind, z, t, target, :] = q
            return 0

        lax.fori_loop(0, TILES, drift, 0)

    def sweep_one(z, _):
        for kind in (0, 1):
            centre, sums = around(q0.at[kind], z, TOP, SPAN)
            for t in range(TILES):
                s = s_buf[kind, z, t, span, :]
                q1[kind, z, t, span, :] = centre[t] * a_buf[kind, z, t, span, :] + (s * s) * sums[t]
        return 0

    lax.fori_loop(1, LAYERS - 1, sweep_one, 0, unroll=5)

    arrived(DOPING)

    def sweep_two(z, _):
        found = []
        for kind in (0, 1):
            centre, sums = around(q1.at[kind], z + DIFFUSION, FIRST, NX)
            n = []
            for t in range(TILES):
                s = s_buf[kind, z + DIFFUSION, t, own, :]
                q = centre[t] * a_buf[kind, z + DIFFUSION, t, own, :] + (s * s) * sums[t]
                n.append(q * rs_buf[kind, z + DIFFUSION, t])
                result[kind, z, t, own, :] = n[t]
            found.append(n)
        for t in range(TILES):
            doping = land[DOP][z, pl.ds(0, NX), pl.ds(128 * t, 128)]
            c_buf[z + CHARGE, t, own, :] = (found[1][t] - found[0][t] + doping) * (0.5 / 6.0)
        return 0

    lax.fori_loop(0, OWN, sweep_two, 0, unroll=4)

    exchange(c_buf, 0, CHARGE, ways, True)

    mine = pl.ds(pl.multiple_of(c * OWN, OWN), OWN)

    def give(index):
        for k in range(TILES // 2):
            there = outs[index].at[mine, :, pl.ds(128 * k, 128)]
            pltpu.make_async_remote_copy(
                src_ref=result.at[index, :, 2 * (1 - c) + k, pl.ds(FIRST, NX), :],
                dst_ref=there,
                send_sem=o_send.at[index, k],
                recv_sem=o_recv.at[index, k],
                device_id=at(0, 0, 1 - c),
                device_id_type=MESH,
            ).start()
            pltpu.make_async_copy(result.at[index, :, 2 * c + k, pl.ds(FIRST, NX), :], there, o_send.at[index, 2 + k]).start()

    give(0)
    give(1)

    exchanged(c_buf, 0, CHARGE, ways)
    exchanged(u2, 1, EARLY, ways)

    def sweep(src, dst, start, stop, unroll, *more):
        def body(z, _):
            _, sums = around(src, z, TOP, SPAN)
            weight = jnp.where(splat(layer_in(z, CHARGE), SPAN), sixth, 0.0)
            for t in range(TILES):
                value = sums[t] * weight + c_buf[z, t, span, :]
                for ref in more:
                    value = value + ref[z, t, span, :]
                dst[z, t, span, :] = value
            return 0

        lax.fori_loop(start, stop, body, 0, unroll=unroll)

    sweep(c_buf, v_a, 1, OWN + 2 * CHARGE - 1, 6, u2)
    sweep(v_a, v_b, 2, OWN + 2 * CHARGE - 2, 5)

    def last_sweep(z, _):
        _, sums = around(v_b, z + CHARGE, FIRST, NX)
        for t in range(TILES):
            result[2, z, t, own, :] = sums[t] * (1.0 / 6.0) + c_buf[z + CHARGE, t, own, :]
        return 0

    lax.fori_loop(0, OWN, last_sweep, 0, unroll=8)
    give(2)

    exchange(c_buf, 0, CHARGE, ways, False)
    exchange(u2, 1, EARLY, ways, False)
    for dz, dx in SIDES:
        when(exists(dz, dx), lambda dz=dz, dx=dx: wait_rows(sent((dz, dx)), in_send.at[3 * dz + dx + 4]))
    for index in range(3):
        view = result.at[index, :, 0, own, :]
        for k in range(TILES // 2):
            for sem in (o_send.at[index, k], o_send.at[index, 2 + k], o_recv.at[index, k]):
                pltpu.make_async_copy(view, view, sem).wait()


def hand_over(*refs):
    ins, outs, sems = refs[:3], refs[3:6], refs[6]
    copies = [pltpu.make_async_copy(ins[k], outs[k], sems.at[k]) for k in range(3)]
    for copy in copies:
        copy.start()
    for copy in copies:
        copy.wait()


def on_device(sizes, *fields):
    most = max(max(sent(side), received(group, core, side)) for side in SIDES for group in range(4) for core in (0, 1))
    landing = [
        pltpu.VMEM(
            (LANDING, 2 * NL) if field in FLAT else (OWN + below + above, LANDING if rows else NX, 2 * NL), fields[field].dtype
        )
        for field, (rows, below, above) in REACH.items()
    ]

    def work(*shape):
        return pltpu.VMEM(shape + (TILES, ROWS, 128), jnp.float32)

    dma = pltpu.SemaphoreType.DMA
    shapes = [jax.ShapeDtypeStruct((NZ, NX, NL), jnp.float32)] * 3
    found = pl.pallas_call(
        lambda *refs: kernel(sizes, *refs),
        out_shape=[pltpu.VMEM((NZ, NX, NL), jnp.float32)] * 3,
        in_specs=[pl.BlockSpec(memory_space=pl.ANY)] * 8,
        out_specs=[pl.BlockSpec(memory_space=pl.ANY)] * 3,
        scratch_shapes=landing
        + [
            work(2, LAYERS),
            pltpu.VMEM((2, LAYERS, TILES, NX, 128), jnp.float32),
            work(2, LAYERS),
            work(2, LAYERS),
            work(2, LAYERS),
            work(3, OWN),
            work(OWN + 2 * CHARGE),
            work(OWN + 2 * CHARGE),
            work(OWN + 2 * CHARGE),
            work(OWN + 2 * CHARGE),
            work(OWN + 2 * EARLY),
            work(OWN + 2 * EARLY),
            pltpu.VMEM((most, 128), jnp.float32),
            pltpu.SemaphoreType.REGULAR,
            dma((9,)),
            dma((4, 9)),
            dma((2, 9)),
            dma((2, 9)),
            dma((3, 4)),
            dma((3, 2)),
        ],
        compiler_params=pltpu.CompilerParams(collective_id=0, has_side_effects=True, vmem_limit_bytes=60 << 20),
    )(*fields)
    return pl.pallas_call(
        hand_over,
        out_shape=shapes,
        in_specs=[pl.BlockSpec(memory_space=pl.ANY)] * 3,
        out_specs=[pl.BlockSpec(memory_space=pl.ANY)] * 3,
        scratch_shapes=[dma((3,))],
        compiler_params=pltpu.CompilerParams(vmem_limit_bytes=8 << 20),
    )(*found)


def solution(mesh):
    sizes = (mesh.shape["gz"], mesh.shape["gx"])
    in_specs = (P("gz", "gx", "gy"),) * 6 + (P("gx", "gy"),) * 2
    out_specs = (P("gz", "gx", "gy"),) * 3

    def step(
        electron_density, hole_density, potential, doping, electron_mobility, hole_mobility, cfl_map, fraction
    ):
        return tuple(
            on_device(
                sizes, electron_density, hole_density, electron_mobility, hole_mobility, potential, doping, cfl_map,
                fraction,
            )
        )

    return jax.shard_map(step, mesh=mesh, in_specs=in_specs, out_specs=out_specs, check_vma=False)
```

```python
import jax
import jax.numpy as jnp
from jax import lax
from jax.experimental import pallas as pl
from jax.experimental.pallas import tpu as pltpu
from jax.sharding import PartitionSpec as P

MESH = pl.DeviceIdType.MESH

CFL_MAX = 8
NZ = 16
NX = 16
NL = 256
OWN = 8
TILES = 4
ROWS = 32
FIRST = 8
LANDING = 24
TOP, SPAN = 4, 24
CHARGE = 3
EARLY = 2
DIFFUSION = 2
UP = CFL_MAX + 1
LAYERS = OWN + 2 * DIFFUSION
SEAM = 8

E, H, ME, MH, PHI, DOP, CFL, FRAC = range(8)
REACH = {
    E: (0, UP, 0),
    H: (0, 0, UP),
    ME: (DIFFUSION, DIFFUSION, DIFFUSION),
    MH: (DIFFUSION, DIFFUSION, DIFFUSION),
    PHI: (EARLY, EARLY, EARLY),
    DOP: (0, 0, 0),
    CFL: (0, 0, 0),
    FRAC: (0, 0, 0),
}
FLAT = (CFL, FRAC)
GROUPS = ((ME, MH), (PHI,), (E, H, CFL, FRAC), (DOP,))
MOBILITIES, POTENTIAL, DENSITIES, DOPING = range(4)
SIDES = [(dz, dx) for dz in (1, -1, 0) for dx in (1, -1, 0)]


def piece(field, core, dz, dx):
    rows, below, above = REACH[field]
    if field in FLAT:
        along_z = (0, 0, 1 if dz == 0 else 0)
    else:
        base = OWN * core - below
        start, stop = base + abs(dx), OWN * core + OWN + above - abs(dx)
        if dz == 0:
            start, stop = max(start, 0), min(stop, NZ)
            along_z = (start, start - base, stop - start)
        elif dz == 1:
            along_z = (NZ + start, start - base, -start)
        else:
            along_z = (0, NZ - base, stop - NZ)
    along_x = {0: (0, 0, NX), 1: (NX - rows, LANDING - rows, rows), -1: (0, NX, rows)}[dx]
    return (along_z, along_x) if along_z[2] > 0 and along_x[2] > 0 else None


def received(group, core, side):
    pieces = [piece(field, core, *side) for field in GROUPS[group]]
    return sum(TILES * p[0][2] * p[1][2] for p in pieces if p is not None)


def sent(side):
    total = 0
    for field in REACH:
        for core in (0, 1):
            p = piece(field, core, *side)
            if p is not None:
                total += TILES // 2 * p[0][2] * p[1][2]
    return total // 2 if side == (0, 0) else total


def kernel(sizes, *refs):
    n_gz, n_gx = sizes
    ins, outs, land = refs[:8], refs[8:11], refs[11:19]
    (s_buf, rs_buf, a_buf, q0, q1, result, c_buf, u2, v_a, v_b, u_a, u_b, count, late, in_send, in_recv, c_send, c_recv,
     o_send, o_recv) = refs[19:]
    g, w, c = lax.axis_index("gz"), lax.axis_index("gx"), lax.axis_index("gy")
    lowest, highest, leftmost, rightmost = g == 0, g == n_gz - 1, w == 0, w == n_gx - 1

    def at(dz, dx, core):
        return (g + dz, w + dx, core)

    def both(*conditions):
        result = None
        for condition in conditions:
            if condition is not None:
                result = condition if result is None else jnp.logical_and(result, condition)
        return result

    def exists(dz, dx):
        return both(
            {1: jnp.logical_not(highest), -1: jnp.logical_not(lowest), 0: None}[dz],
            {1: jnp.logical_not(rightmost), -1: jnp.logical_not(leftmost), 0: None}[dx],
        )

    def when(condition, body):
        if condition is None:
            body()
        else:
            pl.when(condition)(body)

    seam_left = jnp.logical_and(lax.rem(w, SEAM) == 0, jnp.logical_not(leftmost))
    seam_right = jnp.logical_and(lax.rem(w, SEAM) == SEAM - 1, jnp.logical_not(rightmost))
    barrier = pltpu.get_barrier_semaphore()

    def greet(semaphore, dz, dx):
        if (dz, dx) == (0, 0):
            pl.semaphore_signal(semaphore, inc=1, device_id=at(0, 0, 1 - c), device_id_type=MESH)
        else:
            for core in (0, 1):
                pl.semaphore_signal(semaphore, inc=1, device_id=at(dz, dx, core), device_id_type=MESH)

    for dz, dx in SIDES:
        open_side = jnp.logical_not(seam_right) if dx == 1 else None
        when(both(exists(dz, dx), open_side), lambda dz=dz, dx=dx: greet(barrier, dz, dx))
    deep = 3 - lowest.astype(jnp.int32) - highest.astype(jnp.int32)
    wide = 3 - jnp.logical_or(leftmost, seam_left).astype(jnp.int32) - rightmost.astype(jnp.int32)
    pl.semaphore_wait(barrier, 2 * deep * wide - 1)
    for dz in (1, -1, 0):
        when(both(exists(dz, 1), seam_right), lambda dz=dz: greet(late, dz, 1))

    lanes = pl.ds(pl.multiple_of(c * NL, NL), NL)

    def push(group, side):
        dz, dx = side
        for field in GROUPS[group]:
            for core in (0, 1):
                p = piece(field, core, dz, dx)
                if p is None:
                    continue
                (src_z, dst_z, depth), (src_x, dst_x, rows) = p
                if field in FLAT:
                    src = ins[field].at[pl.ds(src_x, rows), :]
                    dst = land[field].at[pl.ds(dst_x, rows), lanes]
                else:
                    src = ins[field].at[pl.ds(src_z, depth), pl.ds(src_x, rows), :]
                    dst = land[field].at[pl.ds(dst_z, depth), pl.ds(dst_x, rows), lanes]
                sem = in_recv.at[group, 3 * dz + dx + 4]

                def remote(src=src, dst=dst, sem=sem, core=core):
                    pltpu.make_async_remote_copy(
                        src_ref=src,
                        dst_ref=dst,
                        send_sem=in_send.at[3 * dz + dx + 4],
                        recv_sem=sem,
                        device_id=at(dz, dx, core),
                        device_id_type=MESH,
                    ).start()

                def local(src=src, dst=dst, sem=sem):
                    pltpu.make_async_copy(src, dst, sem).start()

                if side == (0, 0):
                    pl.when(c == core)(local)
                    pl.when(c != core)(remote)
                else:
                    remote()

    def push_all(group, sides, condition=None):
        for side in sides:
            when(both(exists(*side), condition), lambda side=side: push(group, side))

    def wait_rows(rows, sem):
        view = count.at[pl.ds(0, rows), :]
        pltpu.make_async_copy(view, view, sem).wait()

    def arrived(group, sides=SIDES):
        for dz, dx in sides:
            for core in (0, 1):
                rows = received(group, core, (dz, dx))
                if rows == 0:
                    continue
                even = core == 1 or received(group, 1, (dz, dx)) != rows
                if core == 1 and received(group, 0, (dz, dx)) == rows:
                    continue
                mine = c == core if even else None
                sem = in_recv.at[group, 3 * dz + dx + 4]
                when(both(exists(-dz, -dx), mine), lambda rows=rows, sem=sem: wait_rows(rows, sem))

    right = [(dz, 1) for dz in (1, -1, 0)]
    left = [(dz, -1) for dz in (1, -1, 0)]
    near = [(1, 0), (-1, 0), (0, 0)]
    push_all(DENSITIES, near)
    push_all(MOBILITIES, [(0, 0)])
    for group in (MOBILITIES, POTENTIAL):
        push_all(group, right)
        push_all(group, left, jnp.logical_not(seam_left))
        push_all(group, near[:2])
    push_all(POTENTIAL, [(0, 0)])
    push_all(DOPING, [(0, 0)])

    def splat(flag, rows):
        return jnp.broadcast_to(flag.astype(jnp.int32), (rows, 128)) > 0

    has_left, has_right = jnp.logical_not(leftmost), jnp.logical_not(rightmost)
    row = lax.broadcasted_iota(jnp.int32, (SPAN, 128), 0) + (TOP - FIRST)
    first_row = jnp.where(leftmost, 0, -FIRST)
    last_row = jnp.where(rightmost, NX, NX + FIRST)
    inside = jnp.logical_and(row >= first_row, row < last_row)
    sixth = jnp.where(inside, 1.0 / 6.0, 0.0)
    halo_row = lax.broadcasted_iota(jnp.int32, (8, 128), 0)
    halo_inside = jnp.where(halo_row < 4, has_right.astype(jnp.int32), has_left.astype(jnp.int32))
    lane = lax.broadcasted_iota(jnp.int32, (SPAN, 128), 1)
    at_first, at_last = lane == 0, lane == 127

    def layer_in(z, below):
        z = z - below + OWN * c
        return jnp.logical_and(jnp.logical_or(z >= 0, jnp.logical_not(lowest)), jnp.logical_or(z < NZ, jnp.logical_not(highest)))

    def around(ref, z, start, rows):
        centre = [ref[z, t, pl.ds(start, rows), :] for t in range(TILES)]
        up = [pltpu.roll(v, 127, 1) for v in centre] + [jnp.zeros((rows, 128), jnp.float32)]
        down = [jnp.zeros((rows, 128), jnp.float32)] + [pltpu.roll(v, 1, 1) for v in centre]
        is_first, is_last = at_first[:rows], at_last[:rows]
        sums = []
        for t in range(TILES):
            in_y = jnp.where(is_last, up[t + 1], up[t]) + jnp.where(is_first, down[t], down[t + 1])
            in_z = ref[z + 1, t, pl.ds(start, rows), :] + ref[z - 1, t, pl.ds(start, rows), :]
            in_x = ref[z, t, pl.ds(start + 1, rows), :] + ref[z, t, pl.ds(start - 1, rows), :]
            sums.append((in_z + in_x) + in_y)
        return centre, sums

    def empty(field, start, layers):
        for z in range(start, start + layers):
            land[field][z] = jnp.zeros((NX, 2 * NL), jnp.float32)

    for core in (0, 1):

        @pl.when(jnp.logical_and(lowest, c == core))
        def _(core=core):
            empty(E, 0, UP - OWN * core)

        @pl.when(jnp.logical_and(highest, c == core))
        def _(core=core):
            empty(H, NZ - OWN * core, UP - OWN * (1 - core))

    own, halo = pl.ds(FIRST, NX), pl.ds(NX, 8)
    after, before = pl.ds(FIRST + NX, 8), pl.ds(0, 8)
    above_there, below_there = jnp.logical_or(c == 0, jnp.logical_not(highest)), jnp.logical_or(c == 1, jnp.logical_not(lowest))
    upward, downward = c, c - 1

    def shape(deep, dz, dx):
        return (deep, NX) if dx == 0 else (deep - 1, deep - 1) if dz != 0 else (OWN, deep)

    def exchange(buf, k, deep, ways, start, base=CHARGE, lead=()):
        for dz, dx in ways:
            depth, rows = shape(deep, dz, dx)
            src_z, dst_z = {1: (base + OWN - depth, base - depth), -1: (base, base + OWN), 0: (base, base)}[dz]
            src_x, dst_x = {1: (FIRST + NX - rows, FIRST - rows), -1: (FIRST, FIRST + NX), 0: (FIRST, FIRST)}[dx]
            way = 3 * dz + dx + 4
            chip = {1: upward, -1: downward, 0: 0}[dz]
            core = c if dz == 0 else 1 - c
            src = buf.at[*lead, pl.ds(src_z, depth), :, pl.ds(src_x, rows), :]
            dst = buf.at[*lead, pl.ds(dst_z, depth), :, pl.ds(dst_x, rows), :]

            def one(src=src, dst=dst, way=way, target=at(chip, dx, core)):
                copy = pltpu.make_async_remote_copy(
                    src_ref=src,
                    dst_ref=dst,
                    send_sem=c_send.at[k, way],
                    recv_sem=c_recv.at[k, way],
                    device_id=target,
                    device_id_type=MESH,
                )
                if start:
                    copy.start()
                else:
                    copy.wait_send()

            when(both({1: above_there, -1: below_there, 0: None}[dz], exists(0, dx)), one)

    def exchanged(buf, k, deep, ways, lead=()):
        for dz, dx in ways:
            depth, rows = shape(deep, dz, dx)
            view = buf.at[*lead, pl.ds(0, depth), :, pl.ds(0, rows), :]
            way = 3 * dz + dx + 4

            def one(view=view, way=way):
                pltpu.make_async_copy(view, view, c_recv.at[k, way]).wait()

            when(both({1: below_there, -1: above_there, 0: None}[dz], exists(0, -dx)), one)

    def clear_outside(buf, halo):
        def clear(condition, start, layers, first, rows):
            @pl.when(condition)
            def _():
                for z in range(start, start + layers):
                    buf[z, :, pl.ds(first, rows), :] = jnp.zeros((TILES, rows, 128), jnp.float32)

        clear(jnp.logical_not(below_there), 0, halo, 0, ROWS)
        clear(jnp.logical_not(above_there), halo + OWN, halo, 0, ROWS)
        clear(leftmost, 0, OWN + 2 * halo, TOP, FIRST - TOP)
        clear(rightmost, 0, OWN + 2 * halo, FIRST + NX, FIRST - TOP)

    ways = [(1, 1), (-1, 1), (1, -1), (-1, -1), (0, 1), (0, -1), (1, 0), (-1, 0)]
    for kind in (0, 1):
        clear_outside(q0.at[kind], DIFFUSION)
    clear_outside(u2, CHARGE)
    clear_outside(c_buf, CHARGE)

    arrived(MOBILITIES, [(0, 0)])

    def own_roots(z, there):
        mask = None if there is None else jnp.broadcast_to(there, (NX, 128)) > 0
        for kind, field in ((0, ME), (1, MH)):
            for t in range(TILES):
                m = land[field][z, pl.ds(0, NX), pl.ds(128 * t, 128)]
                rs = lax.rsqrt(m)
                rs_buf[kind, z, t] = rs
                s_buf[kind, z, t, own, :] = m * rs if mask is None else jnp.where(mask, m * rs, 0.0)

    def roots(z, _):
        own_roots(z, None)
        return 0

    lax.fori_loop(DIFFUSION, DIFFUSION + OWN, roots, 0, unroll=4)

    arrived(DENSITIES)
    for half in (0, 1):
        rows, target = pl.ds(8 * half, 8), pl.ds(FIRST + 8 * half, 8)

        def drift(t, _, rows=rows, target=target):
            tile = pl.ds(pl.multiple_of(t * 128, 128), 128)
            d = land[CFL][rows, tile]
            f = land[FRAC][rows, tile]
            rest = 1.0 - f
            bits = [(k, jnp.bitwise_and(d, k) != 0) for k in (8, 4, 2, 1)]
            for kind, field in ((0, E), (1, H)):
                length = OWN + UP
                if kind == 0:
                    v = [land[field][length - 1 - i, rows, tile] for i in range(length)]
                else:
                    v = [land[field][i, rows, tile] for i in range(length)]
                for k, bit in bits:
                    if k == 8:
                        v = [jnp.where(bit, v[i + 8], v[i]) if i <= OWN else v[i] for i in range(length - 1)]
                    else:
                        v = [jnp.where(bit, v[i + k], v[i]) for i in range(len(v) - k)]
                for i in range(OWN):
                    z = DIFFUSION + (OWN - 1 - i if kind == 0 else i)
                    q0[kind, z, t, target, :] = (rest * v[i] + f * v[i + 1]) * s_buf[kind, z, t, target, :]
            return 0

        lax.fori_loop(0, TILES, drift, 0, unroll=2)

    @pl.when(seam_left)
    def _():
        pl.semaphore_wait(late, 2 * deep)
        for group in (MOBILITIES, POTENTIAL):
            push_all(group, left)

    kinds = (slice(None),)
    exchange(q0, 2, DIFFUSION, ways, True, DIFFUSION, kinds)

    arrived(MOBILITIES, SIDES[:-1])
    for z in (*range(DIFFUSION), *range(DIFFUSION + OWN, LAYERS)):
        own_roots(z, layer_in(z, DIFFUSION).astype(jnp.int32))

    def halo_roots(z, _):
        mask = halo_inside * layer_in(z, DIFFUSION).astype(jnp.int32) > 0
        for kind, field in ((0, ME), (1, MH)):
            for t in range(TILES):
                m = land[field][z, halo, pl.ds(128 * t, 128)]
                s = jnp.where(mask, m * lax.rsqrt(m), 0.0)
                s_buf[kind, z, t, before, :] = s
                s_buf[kind, z, t, after, :] = s
        return 0

    lax.fori_loop(0, LAYERS, halo_roots, 0, unroll=4)

    def stays(z, _):
        for kind in (0, 1):
            centre, sums = around(s_buf.at[kind], z, TOP, SPAN)
            for t in range(TILES):
                a_buf[kind, z, t, pl.ds(TOP, SPAN), :] = 1.0 - centre[t] * sums[t]
        return 0

    lax.fori_loop(1, LAYERS - 1, stays, 0, unroll=5)

    arrived(POTENTIAL)

    def spread(z, _):
        in_z = layer_in(z, EARLY).astype(jnp.int32)
        own_mask, halo_mask = jnp.broadcast_to(in_z, (NX, 128)) > 0, halo_inside * in_z > 0
        for t in range(TILES):
            tile = pl.ds(128 * t, 128)
            u_a[z, t, own, :] = jnp.where(own_mask, land[PHI][z, pl.ds(0, NX), tile], 0.0)
            phi = jnp.where(halo_mask, land[PHI][z, halo, tile], 0.0)
            u_a[z, t, before, :] = phi
            u_a[z, t, after, :] = phi
        return 0

    lax.fori_loop(0, OWN + 2 * EARLY, spread, 0, unroll=2)

    span = pl.ds(TOP, SPAN)

    def first_sweep(z, _):
        _, sums = around(u_a, z, TOP, SPAN)
        weight = jnp.where(splat(layer_in(z, EARLY), SPAN), sixth, 0.0)
        for t in range(TILES):
            u_b[z, t, span, :] = sums[t] * weight
        return 0

    lax.fori_loop(1, OWN + 2 * EARLY - 1, first_sweep, 0, unroll=5)

    def second_sweep(z, _):
        _, sums = around(u_b, z + EARLY, FIRST, NX)
        for t in range(TILES):
            u2[z + CHARGE, t, own, :] = sums[t] * (1.0 / 6.0)
        return 0

    lax.fori_loop(0, OWN, second_sweep, 0, unroll=4)
    exchange(u2, 1, EARLY, ways, True)

    exchanged(q0, 2, DIFFUSION, ways, kinds)
    def sweep_one(z, _):
        for kind in (0, 1):
            centre, sums = around(q0.at[kind], z, TOP, SPAN)
            for t in range(TILES):
                s = s_buf[kind, z, t, span, :]
                q1[kind, z, t, span, :] = centre[t] * a_buf[kind, z, t, span, :] + (s * s) * sums[t]
        return 0

    lax.fori_loop(1, LAYERS - 1, sweep_one, 0, unroll=5)

    arrived(DOPING)

    def sweep_two(z, _):
        found = []
        for kind in (0, 1):
            centre, sums = around(q1.at[kind], z + DIFFUSION, FIRST, NX)
            n = []
            for t in range(TILES):
                s = s_buf[kind, z + DIFFUSION, t, own, :]
                q = centre[t] * a_buf[kind, z + DIFFUSION, t, own, :] + (s * s) * sums[t]
                n.append(q * rs_buf[kind, z + DIFFUSION, t])
                result[kind, z, t, own, :] = n[t]
            found.append(n)
        for t in range(TILES):
            doping = land[DOP][z, pl.ds(0, NX), pl.ds(128 * t, 128)]
            c_buf[z + CHARGE, t, own, :] = (found[1][t] - found[0][t] + doping) * (0.5 / 6.0)
        return 0

    lax.fori_loop(0, OWN, sweep_two, 0, unroll=4)

    exchange(c_buf, 0, CHARGE, ways, True)

    mine = pl.ds(pl.multiple_of(c * OWN, OWN), OWN)

    def give(index):
        for k in range(TILES // 2):
            there = outs[index].at[mine, :, pl.ds(128 * k, 128)]
            pltpu.make_async_remote_copy(
                src_ref=result.at[index, :, 2 * (1 - c) + k, pl.ds(FIRST, NX), :],
                dst_ref=there,
                send_sem=o_send.at[index, k],
                recv_sem=o_recv.at[index, k],
                device_id=at(0, 0, 1 - c),
                device_id_type=MESH,
            ).start()
            pltpu.make_async_copy(result.at[index, :, 2 * c + k, pl.ds(FIRST, NX), :], there, o_send.at[index, 2 + k]).start()

    give(0)
    give(1)

    exchanged(c_buf, 0, CHARGE, ways)
    exchanged(u2, 1, EARLY, ways)

    def sweep(src, dst, start, stop, unroll, *more):
        def body(z, _):
            _, sums = around(src, z, TOP, SPAN)
            weight = jnp.where(splat(layer_in(z, CHARGE), SPAN), sixth, 0.0)
            for t in range(TILES):
                value = sums[t] * weight + c_buf[z, t, span, :]
                for ref in more:
                    value = value + ref[z, t, span, :]
                dst[z, t, span, :] = value
            return 0

        lax.fori_loop(start, stop, body, 0, unroll=unroll)

    sweep(c_buf, v_a, 1, OWN + 2 * CHARGE - 1, 6, u2)
    sweep(v_a, v_b, 2, OWN + 2 * CHARGE - 2, 5)

    def last_sweep(z, _):
        _, sums = around(v_b, z + CHARGE, FIRST, NX)
        for t in range(TILES):
            result[2, z, t, own, :] = sums[t] * (1.0 / 6.0) + c_buf[z + CHARGE, t, own, :]
        return 0

    lax.fori_loop(0, OWN, last_sweep, 0, unroll=8)
    give(2)

    exchange(c_buf, 0, CHARGE, ways, False)
    exchange(u2, 1, EARLY, ways, False)
    exchange(q0, 2, DIFFUSION, ways, False, DIFFUSION, kinds)
    for dz, dx in SIDES:
        when(exists(dz, dx), lambda dz=dz, dx=dx: wait_rows(sent((dz, dx)), in_send.at[3 * dz + dx + 4]))
    for index in range(3):
        view = result.at[index, :, 0, own, :]
        for k in range(TILES // 2):
            for sem in (o_send.at[index, k], o_send.at[index, 2 + k], o_recv.at[index, k]):
                pltpu.make_async_copy(view, view, sem).wait()


def hand_over(*refs):
    ins, outs, sems = refs[:3], refs[3:6], refs[6]
    copies = [pltpu.make_async_copy(ins[k], outs[k], sems.at[k]) for k in range(3)]
    for copy in copies:
        copy.start()
    for copy in copies:
        copy.wait()


def on_device(sizes, *fields):
    most = max(max(sent(side), received(group, core, side)) for side in SIDES for group in range(4) for core in (0, 1))
    landing = [
        pltpu.VMEM(
            (LANDING, 2 * NL) if field in FLAT else (OWN + below + above, LANDING if rows else NX, 2 * NL), fields[field].dtype
        )
        for field, (rows, below, above) in REACH.items()
    ]

    def work(*shape):
        return pltpu.VMEM(shape + (TILES, ROWS, 128), jnp.float32)

    dma = pltpu.SemaphoreType.DMA
    shapes = [jax.ShapeDtypeStruct((NZ, NX, NL), jnp.float32)] * 3
    found = pl.pallas_call(
        lambda *refs: kernel(sizes, *refs),
        out_shape=[pltpu.VMEM((NZ, NX, NL), jnp.float32)] * 3,
        in_specs=[pl.BlockSpec(memory_space=pl.ANY)] * 8,
        out_specs=[pl.BlockSpec(memory_space=pl.ANY)] * 3,
        scratch_shapes=landing
        + [
            work(2, LAYERS),
            pltpu.VMEM((2, LAYERS, TILES, NX, 128), jnp.float32),
            work(2, LAYERS),
            work(2, LAYERS),
            work(2, LAYERS),
            work(3, OWN),
            work(OWN + 2 * CHARGE),
            work(OWN + 2 * CHARGE),
            work(OWN + 2 * CHARGE),
            work(OWN + 2 * CHARGE),
            work(OWN + 2 * EARLY),
            work(OWN + 2 * EARLY),
            pltpu.VMEM((most, 128), jnp.float32),
            pltpu.SemaphoreType.REGULAR,
            dma((9,)),
            dma((4, 9)),
            dma((3, 9)),
            dma((3, 9)),
            dma((3, 4)),
            dma((3, 2)),
        ],
        compiler_params=pltpu.CompilerParams(collective_id=0, has_side_effects=True, vmem_limit_bytes=60 << 20),
    )(*fields)
    return pl.pallas_call(
        hand_over,
        out_shape=shapes,
        in_specs=[pl.BlockSpec(memory_space=pl.ANY)] * 3,
        out_specs=[pl.BlockSpec(memory_space=pl.ANY)] * 3,
        scratch_shapes=[dma((3,))],
        compiler_params=pltpu.CompilerParams(vmem_limit_bytes=8 << 20),
    )(*found)


def solution(mesh):
    sizes = (mesh.shape["gz"], mesh.shape["gx"])
    in_specs = (P("gz", "gx", "gy"),) * 6 + (P("gx", "gy"),) * 2
    out_specs = (P("gz", "gx", "gy"),) * 3

    def step(
        electron_density, hole_density, potential, doping, electron_mobility, hole_mobility, cfl_map, fraction
    ):
        return tuple(
            on_device(
                sizes, electron_density, hole_density, electron_mobility, hole_mobility, potential, doping, cfl_map,
                fraction,
            )
        )

    return jax.shard_map(step, mesh=mesh, in_specs=in_specs, out_specs=out_specs, check_vma=False)
```

```python
import jax
import jax.numpy as jnp
from jax import lax
from jax.experimental import pallas as pl
from jax.experimental.pallas import tpu as pltpu
from jax.sharding import PartitionSpec as P

MESH = pl.DeviceIdType.MESH

CFL_MAX = 8
NZ = 16
NX = 16
NL = 256
OWN = 8
TILES = 4
ROWS = 32
FIRST = 8
LANDING = 24
TOP, SPAN = 4, 24
CHARGE = 3
EARLY = 2
DIFFUSION = 2
UP = CFL_MAX + 1
LAYERS = OWN + 2 * DIFFUSION
SEAM = 8

E, H, ME, MH, PHI, DOP, CFL, FRAC = range(8)
REACH = {
    E: (0, UP, 0),
    H: (0, 0, UP),
    ME: (DIFFUSION, DIFFUSION, DIFFUSION),
    MH: (DIFFUSION, DIFFUSION, DIFFUSION),
    PHI: (EARLY, EARLY, EARLY),
    DOP: (0, 0, 0),
    CFL: (0, 0, 0),
    FRAC: (0, 0, 0),
}
FLAT = (CFL, FRAC)
GROUPS = ((ME, MH), (PHI,), (E, H, CFL, FRAC), (DOP,))
MOBILITIES, POTENTIAL, DENSITIES, DOPING = range(4)
SIDES = [(dz, dx) for dz in (1, -1, 0) for dx in (1, -1, 0)]


def piece(field, core, dz, dx):
    rows, below, above = REACH[field]
    if field in FLAT:
        along_z = (0, 0, 1 if dz == 0 else 0)
    else:
        base = OWN * core - below
        start, stop = base + abs(dx), OWN * core + OWN + above - abs(dx)
        if dz == 0:
            start, stop = max(start, 0), min(stop, NZ)
            along_z = (start, start - base, stop - start)
        elif dz == 1:
            along_z = (NZ + start, start - base, -start)
        else:
            along_z = (0, NZ - base, stop - NZ)
    along_x = {0: (0, 0, NX), 1: (NX - rows, LANDING - rows, rows), -1: (0, NX, rows)}[dx]
    return (along_z, along_x) if along_z[2] > 0 and along_x[2] > 0 else None


def received(group, core, side):
    pieces = [piece(field, core, *side) for field in GROUPS[group]]
    return sum(TILES * p[0][2] * p[1][2] for p in pieces if p is not None)


def sent(side):
    total = 0
    for field in REACH:
        for core in (0, 1):
            p = piece(field, core, *side)
            if p is not None:
                total += TILES // 2 * p[0][2] * p[1][2]
    return total // 2 if side == (0, 0) else total


def kernel(sizes, *refs):
    n_gz, n_gx = sizes
    ins, outs, land = refs[:8], refs[8:11], refs[11:19]
    (s_buf, rs_buf, a_buf, q0, q1, result, c_buf, u2, v_a, v_b, u_a, u_b, count, late, in_send, in_recv, c_send, c_recv,
     o_send, o_recv) = refs[19:]
    g, w, c = lax.axis_index("gz"), lax.axis_index("gx"), lax.axis_index("gy")
    lowest, highest, leftmost, rightmost = g == 0, g == n_gz - 1, w == 0, w == n_gx - 1

    def at(dz, dx, core):
        return (g + dz, w + dx, core)

    def both(*conditions):
        result = None
        for condition in conditions:
            if condition is not None:
                result = condition if result is None else jnp.logical_and(result, condition)
        return result

    def exists(dz, dx):
        return both(
            {1: jnp.logical_not(highest), -1: jnp.logical_not(lowest), 0: None}[dz],
            {1: jnp.logical_not(rightmost), -1: jnp.logical_not(leftmost), 0: None}[dx],
        )

    def when(condition, body):
        if condition is None:
            body()
        else:
            pl.when(condition)(body)

    seam_left = jnp.logical_and(lax.rem(w, SEAM) == 0, jnp.logical_not(leftmost))
    seam_right = jnp.logical_and(lax.rem(w, SEAM) == SEAM - 1, jnp.logical_not(rightmost))
    barrier = pltpu.get_barrier_semaphore()

    def greet(semaphore, dz, dx):
        if (dz, dx) == (0, 0):
            pl.semaphore_signal(semaphore, inc=1, device_id=at(0, 0, 1 - c), device_id_type=MESH)
        else:
            for core in (0, 1):
                pl.semaphore_signal(semaphore, inc=1, device_id=at(dz, dx, core), device_id_type=MESH)

    for dz, dx in SIDES:
        open_side = jnp.logical_not(seam_right) if dx == 1 else None
        when(both(exists(dz, dx), open_side), lambda dz=dz, dx=dx: greet(barrier, dz, dx))
    deep = 3 - lowest.astype(jnp.int32) - highest.astype(jnp.int32)
    wide = 3 - jnp.logical_or(leftmost, seam_left).astype(jnp.int32) - rightmost.astype(jnp.int32)
    pl.semaphore_wait(barrier, 2 * deep * wide - 1)
    for dz in (1, -1, 0):
        when(both(exists(dz, 1), seam_right), lambda dz=dz: greet(late, dz, 1))

    lanes = pl.ds(pl.multiple_of(c * NL, NL), NL)

    def push(group, side):
        dz, dx = side
        for field in GROUPS[group]:
            for core in (0, 1):
                p = piece(field, core, dz, dx)
                if p is None:
                    continue
                (src_z, dst_z, depth), (src_x, dst_x, rows) = p
                if field in FLAT:
                    src = ins[field].at[pl.ds(src_x, rows), :]
                    dst = land[field].at[pl.ds(dst_x, rows), lanes]
                else:
                    src = ins[field].at[pl.ds(src_z, depth), pl.ds(src_x, rows), :]
                    dst = land[field].at[pl.ds(dst_z, depth), pl.ds(dst_x, rows), lanes]
                sem = in_recv.at[group, 3 * dz + dx + 4]

                def remote(src=src, dst=dst, sem=sem, core=core):
                    pltpu.make_async_remote_copy(
                        src_ref=src,
                        dst_ref=dst,
                        send_sem=in_send.at[3 * dz + dx + 4],
                        recv_sem=sem,
                        device_id=at(dz, dx, core),
                        device_id_type=MESH,
                    ).start()

                def local(src=src, dst=dst, sem=sem):
                    pltpu.make_async_copy(src, dst, sem).start()

                if side == (0, 0):
                    pl.when(c == core)(local)
                    pl.when(c != core)(remote)
                else:
                    remote()

    def push_all(group, sides, condition=None):
        for side in sides:
            when(both(exists(*side), condition), lambda side=side: push(group, side))

    def wait_rows(rows, sem):
        view = count.at[pl.ds(0, rows), :]
        pltpu.make_async_copy(view, view, sem).wait()

    def arrived(group, sides=SIDES):
        for dz, dx in sides:
            for core in (0, 1):
                rows = received(group, core, (dz, dx))
                if rows == 0:
                    continue
                even = core == 1 or received(group, 1, (dz, dx)) != rows
                if core == 1 and received(group, 0, (dz, dx)) == rows:
                    continue
                mine = c == core if even else None
                sem = in_recv.at[group, 3 * dz + dx + 4]
                when(both(exists(-dz, -dx), mine), lambda rows=rows, sem=sem: wait_rows(rows, sem))

    right = [(dz, 1) for dz in (1, -1, 0)]
    left = [(dz, -1) for dz in (1, -1, 0)]
    near = [(1, 0), (-1, 0), (0, 0)]
    push_all(DENSITIES, near)
    push_all(MOBILITIES, [(0, 0)])
    for group in (MOBILITIES, POTENTIAL):
        push_all(group, right)
        push_all(group, left, jnp.logical_not(seam_left))
        push_all(group, near[:2])
    push_all(POTENTIAL, [(0, 0)])
    push_all(DOPING, [(0, 0)])

    def splat(flag, rows):
        return jnp.broadcast_to(flag.astype(jnp.int32), (rows, 128)) > 0

    has_left, has_right = jnp.logical_not(leftmost), jnp.logical_not(rightmost)
    row = lax.broadcasted_iota(jnp.int32, (SPAN, 128), 0) + (TOP - FIRST)
    first_row = jnp.where(leftmost, 0, -FIRST)
    last_row = jnp.where(rightmost, NX, NX + FIRST)
    inside = jnp.logical_and(row >= first_row, row < last_row)
    sixth = jnp.where(inside, 1.0 / 6.0, 0.0)
    halo_row = lax.broadcasted_iota(jnp.int32, (8, 128), 0)
    halo_inside = jnp.where(halo_row < 4, has_right.astype(jnp.int32), has_left.astype(jnp.int32))
    lane = lax.broadcasted_iota(jnp.int32, (SPAN, 128), 1)
    at_first, at_last = lane == 0, lane == 127

    def layer_in(z, below):
        z = z - below + OWN * c
        return jnp.logical_and(jnp.logical_or(z >= 0, jnp.logical_not(lowest)), jnp.logical_or(z < NZ, jnp.logical_not(highest)))

    def around(ref, z, start, rows):
        centre = [ref[z, t, pl.ds(start, rows), :] for t in range(TILES)]
        up = [pltpu.roll(v, 127, 1) for v in centre] + [jnp.zeros((rows, 128), jnp.float32)]
        down = [jnp.zeros((rows, 128), jnp.float32)] + [pltpu.roll(v, 1, 1) for v in centre]
        is_first, is_last = at_first[:rows], at_last[:rows]
        sums = []
        for t in range(TILES):
            in_y = jnp.where(is_last, up[t + 1], up[t]) + jnp.where(is_first, down[t], down[t + 1])
            in_z = ref[z + 1, t, pl.ds(start, rows), :] + ref[z - 1, t, pl.ds(start, rows), :]
            in_x = ref[z, t, pl.ds(start + 1, rows), :] + ref[z, t, pl.ds(start - 1, rows), :]
            sums.append((in_z + in_x) + in_y)
        return centre, sums

    def empty(field, start, layers):
        for z in range(start, start + layers):
            land[field][z] = jnp.zeros((NX, 2 * NL), jnp.float32)

    for core in (0, 1):

        @pl.when(jnp.logical_and(lowest, c == core))
        def _(core=core):
            empty(E, 0, UP - OWN * core)

        @pl.when(jnp.logical_and(highest, c == core))
        def _(core=core):
            empty(H, NZ - OWN * core, UP - OWN * (1 - core))

    own, halo = pl.ds(FIRST, NX), pl.ds(NX, 8)
    after, before = pl.ds(FIRST + NX, 8), pl.ds(0, 8)
    above_there, below_there = jnp.logical_or(c == 0, jnp.logical_not(highest)), jnp.logical_or(c == 1, jnp.logical_not(lowest))
    upward, downward = c, c - 1

    def shape(deep, dz, dx):
        return (deep, NX) if dx == 0 else (deep - 1, deep - 1) if dz != 0 else (OWN, deep)

    def exchange(buf, k, deep, ways, start, base=CHARGE, lead=()):
        for dz, dx in ways:
            depth, rows = shape(deep, dz, dx)
            src_z, dst_z = {1: (base + OWN - depth, base - depth), -1: (base, base + OWN), 0: (base, base)}[dz]
            src_x, dst_x = {1: (FIRST + NX - rows, FIRST - rows), -1: (FIRST, FIRST + NX), 0: (FIRST, FIRST)}[dx]
            way = 3 * dz + dx + 4
            chip = {1: upward, -1: downward, 0: 0}[dz]
            core = c if dz == 0 else 1 - c
            src = buf.at[*lead, pl.ds(src_z, depth), :, pl.ds(src_x, rows), :]
            dst = buf.at[*lead, pl.ds(dst_z, depth), :, pl.ds(dst_x, rows), :]

            def one(src=src, dst=dst, way=way, target=at(chip, dx, core)):
                copy = pltpu.make_async_remote_copy(
                    src_ref=src,
                    dst_ref=dst,
                    send_sem=c_send.at[k, way],
                    recv_sem=c_recv.at[k, way],
                    device_id=target,
                    device_id_type=MESH,
                )
                if start:
                    copy.start()
                else:
                    copy.wait_send()

            when(both({1: above_there, -1: below_there, 0: None}[dz], exists(0, dx)), one)

    def exchanged(buf, k, deep, ways, lead=()):
        for dz, dx in ways:
            depth, rows = shape(deep, dz, dx)
            view = buf.at[*lead, pl.ds(0, depth), :, pl.ds(0, rows), :]
            way = 3 * dz + dx + 4

            def one(view=view, way=way):
                pltpu.make_async_copy(view, view, c_recv.at[k, way]).wait()

            when(both({1: below_there, -1: above_there, 0: None}[dz], exists(0, -dx)), one)

    def clear_outside(buf, halo):
        def clear(condition, start, layers, first, rows):
            @pl.when(condition)
            def _():
                for z in range(start, start + layers):
                    buf[z, :, pl.ds(first, rows), :] = jnp.zeros((TILES, rows, 128), jnp.float32)

        clear(jnp.logical_not(below_there), 0, halo, 0, ROWS)
        clear(jnp.logical_not(above_there), halo + OWN, halo, 0, ROWS)
        clear(leftmost, 0, OWN + 2 * halo, TOP, FIRST - TOP)
        clear(rightmost, 0, OWN + 2 * halo, FIRST + NX, FIRST - TOP)

    to_right = [(1, 1), (-1, 1), (0, 1)]
    to_others = [(1, -1), (-1, -1), (0, -1), (1, 0), (-1, 0)]
    ways = to_right + to_others
    for kind in (0, 1):
        clear_outside(q0.at[kind], DIFFUSION)
    clear_outside(u2, CHARGE)
    clear_outside(c_buf, CHARGE)

    arrived(MOBILITIES, [(0, 0)])

    def own_roots(z, there):
        mask = None if there is None else jnp.broadcast_to(there, (NX, 128)) > 0
        for kind, field in ((0, ME), (1, MH)):
            for t in range(TILES):
                m = land[field][z, pl.ds(0, NX), pl.ds(128 * t, 128)]
                rs = lax.rsqrt(m)
                rs_buf[kind, z, t] = rs
                s_buf[kind, z, t, own, :] = m * rs if mask is None else jnp.where(mask, m * rs, 0.0)

    def roots(z, _):
        own_roots(z, None)
        return 0

    lax.fori_loop(DIFFUSION, DIFFUSION + OWN, roots, 0, unroll=4)

    arrived(DENSITIES)
    kinds = (slice(None),)
    for half in (1, 0):
        rows, target = pl.ds(8 * half, 8), pl.ds(FIRST + 8 * half, 8)

        def drift(t, _, rows=rows, target=target):
            tile = pl.ds(pl.multiple_of(t * 128, 128), 128)
            d = land[CFL][rows, tile]
            f = land[FRAC][rows, tile]
            rest = 1.0 - f
            bits = [(k, jnp.bitwise_and(d, k) != 0) for k in (8, 4, 2, 1)]
            for kind, field in ((0, E), (1, H)):
                length = OWN + UP
                if kind == 0:
                    v = [land[field][length - 1 - i, rows, tile] for i in range(length)]
                else:
                    v = [land[field][i, rows, tile] for i in range(length)]
                for k, bit in bits:
                    if k == 8:
                        v = [jnp.where(bit, v[i + 8], v[i]) if i <= OWN else v[i] for i in range(length - 1)]
                    else:
                        v = [jnp.where(bit, v[i + k], v[i]) for i in range(len(v) - k)]
                for i in range(OWN):
                    z = DIFFUSION + (OWN - 1 - i if kind == 0 else i)
                    q0[kind, z, t, target, :] = (rest * v[i] + f * v[i + 1]) * s_buf[kind, z, t, target, :]
            return 0

        lax.fori_loop(0, TILES, drift, 0, unroll=2)
        if half == 1:
            exchange(q0, 2, DIFFUSION, to_right, True, DIFFUSION, kinds)

    @pl.when(seam_left)
    def _():
        pl.semaphore_wait(late, 2 * deep)
        for group in (MOBILITIES, POTENTIAL):
            push_all(group, left)

    exchange(q0, 2, DIFFUSION, to_others, True, DIFFUSION, kinds)

    arrived(POTENTIAL)

    def spread(z, _):
        in_z = layer_in(z, EARLY).astype(jnp.int32)
        own_mask, halo_mask = jnp.broadcast_to(in_z, (NX, 128)) > 0, halo_inside * in_z > 0
        for t in range(TILES):
            tile = pl.ds(128 * t, 128)
            u_a[z, t, own, :] = jnp.where(own_mask, land[PHI][z, pl.ds(0, NX), tile], 0.0)
            phi = jnp.where(halo_mask, land[PHI][z, halo, tile], 0.0)
            u_a[z, t, before, :] = phi
            u_a[z, t, after, :] = phi
        return 0

    lax.fori_loop(0, OWN + 2 * EARLY, spread, 0, unroll=2)

    span = pl.ds(TOP, SPAN)

    def first_sweep(z, _):
        _, sums = around(u_a, z, TOP, SPAN)
        weight = jnp.where(splat(layer_in(z, EARLY), SPAN), sixth, 0.0)
        for t in range(TILES):
            u_b[z, t, span, :] = sums[t] * weight
        return 0

    lax.fori_loop(1, OWN + 2 * EARLY - 1, first_sweep, 0, unroll=5)

    def second_sweep(z, _):
        _, sums = around(u_b, z + EARLY, FIRST, NX)
        for t in range(TILES):
            u2[z + CHARGE, t, own, :] = sums[t] * (1.0 / 6.0)
        return 0

    lax.fori_loop(0, OWN, second_sweep, 0, unroll=4)
    exchange(u2, 1, EARLY, ways, True)

    arrived(MOBILITIES, SIDES[:-1])
    for z in (*range(DIFFUSION), *range(DIFFUSION + OWN, LAYERS)):
        own_roots(z, layer_in(z, DIFFUSION).astype(jnp.int32))

    def halo_roots(z, _):
        mask = halo_inside * layer_in(z, DIFFUSION).astype(jnp.int32) > 0
        for kind, field in ((0, ME), (1, MH)):
            for t in range(TILES):
                m = land[field][z, halo, pl.ds(128 * t, 128)]
                s = jnp.where(mask, m * lax.rsqrt(m), 0.0)
                s_buf[kind, z, t, before, :] = s
                s_buf[kind, z, t, after, :] = s
        return 0

    lax.fori_loop(0, LAYERS, halo_roots, 0, unroll=4)

    def stays(z, _):
        for kind in (0, 1):
            centre, sums = around(s_buf.at[kind], z, TOP, SPAN)
            for t in range(TILES):
                a_buf[kind, z, t, pl.ds(TOP, SPAN), :] = 1.0 - centre[t] * sums[t]
        return 0

    lax.fori_loop(1, LAYERS - 1, stays, 0, unroll=5)

    exchanged(q0, 2, DIFFUSION, ways, kinds)
    def sweep_one(z, _):
        for kind in (0, 1):
            centre, sums = around(q0.at[kind], z, TOP, SPAN)
            for t in range(TILES):
                s = s_buf[kind, z, t, span, :]
                q1[kind, z, t, span, :] = centre[t] * a_buf[kind, z, t, span, :] + (s * s) * sums[t]
        return 0

    lax.fori_loop(1, LAYERS - 1, sweep_one, 0, unroll=5)

    arrived(DOPING)

    for half in (1, 0):
        part = pl.ds(FIRST + 8 * half, 8)

        def sweep_two(z, _, half=half, part=part):
            found = []
            for kind in (0, 1):
                centre, sums = around(q1.at[kind], z + DIFFUSION, FIRST + 8 * half, 8)
                n = []
                for t in range(TILES):
                    s = s_buf[kind, z + DIFFUSION, t, part, :]
                    q = centre[t] * a_buf[kind, z + DIFFUSION, t, part, :] + (s * s) * sums[t]
                    n.append(q * rs_buf[kind, z + DIFFUSION, t, pl.ds(8 * half, 8), :])
                    result[kind, z, t, part, :] = n[t]
                found.append(n)
            for t in range(TILES):
                doping = land[DOP][z, pl.ds(8 * half, 8), pl.ds(128 * t, 128)]
                c_buf[z + CHARGE, t, part, :] = (found[1][t] - found[0][t] + doping) * (0.5 / 6.0)
            return 0

        lax.fori_loop(0, OWN, sweep_two, 0, unroll=8)
        exchange(c_buf, 0, CHARGE, to_right if half == 1 else to_others, True)

    def give(index, first=0, layers=OWN):
        mine, part = pl.ds(c * OWN + first, layers), pl.ds(first, layers)
        for k in range(TILES // 2):
            there = outs[index].at[mine, :, pl.ds(128 * k, 128)]
            pltpu.make_async_remote_copy(
                src_ref=result.at[index, part, 2 * (1 - c) + k, pl.ds(FIRST, NX), :],
                dst_ref=there,
                send_sem=o_send.at[index, k],
                recv_sem=o_recv.at[index, k],
                device_id=at(0, 0, 1 - c),
                device_id_type=MESH,
            ).start()
            pltpu.make_async_copy(result.at[index, part, 2 * c + k, pl.ds(FIRST, NX), :], there, o_send.at[index, 2 + k]).start()

    give(0)
    give(1)

    exchanged(c_buf, 0, CHARGE, ways)
    exchanged(u2, 1, EARLY, ways)

    def sweep(src, dst, start, stop, unroll, *more):
        def body(z, _):
            _, sums = around(src, z, TOP, SPAN)
            weight = jnp.where(splat(layer_in(z, CHARGE), SPAN), sixth, 0.0)
            for t in range(TILES):
                value = sums[t] * weight + c_buf[z, t, span, :]
                for ref in more:
                    value = value + ref[z, t, span, :]
                dst[z, t, span, :] = value
            return 0

        lax.fori_loop(start, stop, body, 0, unroll=unroll)

    sweep(c_buf, v_a, 1, OWN + 2 * CHARGE - 1, 6, u2)
    sweep(v_a, v_b, 2, OWN + 2 * CHARGE - 2, 5)

    def last_sweep(z, _):
        _, sums = around(v_b, z + CHARGE, FIRST, NX)
        for t in range(TILES):
            result[2, z, t, own, :] = sums[t] * (1.0 / 6.0) + c_buf[z + CHARGE, t, own, :]
        return 0

    for first in (0, OWN // 2):
        lax.fori_loop(first, first + OWN // 2, last_sweep, 0, unroll=4)
        give(2, first, OWN // 2)

    exchange(c_buf, 0, CHARGE, ways, False)
    exchange(u2, 1, EARLY, ways, False)
    exchange(q0, 2, DIFFUSION, ways, False, DIFFUSION, kinds)
    for dz, dx in SIDES:
        when(exists(dz, dx), lambda dz=dz, dx=dx: wait_rows(sent((dz, dx)), in_send.at[3 * dz + dx + 4]))
    for index in range(3):
        view = result.at[index, :, 0, own, :]
        for k in range(TILES // 2):
            for sem in (o_send.at[index, k], o_send.at[index, 2 + k], o_recv.at[index, k]):
                pltpu.make_async_copy(view, view, sem).wait()


def hand_over(*refs):
    ins, outs, sems = refs[:3], refs[3:6], refs[6]
    copies = [pltpu.make_async_copy(ins[k], outs[k], sems.at[k]) for k in range(3)]
    for copy in copies:
        copy.start()
    for copy in copies:
        copy.wait()


def on_device(sizes, *fields):
    most = max(max(sent(side), received(group, core, side)) for side in SIDES for group in range(4) for core in (0, 1))
    landing = [
        pltpu.VMEM(
            (LANDING, 2 * NL) if field in FLAT else (OWN + below + above, LANDING if rows else NX, 2 * NL), fields[field].dtype
        )
        for field, (rows, below, above) in REACH.items()
    ]

    def work(*shape):
        return pltpu.VMEM(shape + (TILES, ROWS, 128), jnp.float32)

    dma = pltpu.SemaphoreType.DMA
    shapes = [jax.ShapeDtypeStruct((NZ, NX, NL), jnp.float32)] * 3
    found = pl.pallas_call(
        lambda *refs: kernel(sizes, *refs),
        out_shape=[pltpu.VMEM((NZ, NX, NL), jnp.float32)] * 3,
        in_specs=[pl.BlockSpec(memory_space=pl.ANY)] * 8,
        out_specs=[pl.BlockSpec(memory_space=pl.ANY)] * 3,
        scratch_shapes=landing
        + [
            work(2, LAYERS),
            pltpu.VMEM((2, LAYERS, TILES, NX, 128), jnp.float32),
            work(2, LAYERS),
            work(2, LAYERS),
            work(2, LAYERS),
            work(3, OWN),
            work(OWN + 2 * CHARGE),
            work(OWN + 2 * CHARGE),
            work(OWN + 2 * CHARGE),
            work(OWN + 2 * CHARGE),
            work(OWN + 2 * EARLY),
            work(OWN + 2 * EARLY),
            pltpu.VMEM((most, 128), jnp.float32),
            pltpu.SemaphoreType.REGULAR,
            dma((9,)),
            dma((4, 9)),
            dma((3, 9)),
            dma((3, 9)),
            dma((3, 4)),
            dma((3, 2)),
        ],
        compiler_params=pltpu.CompilerParams(collective_id=0, has_side_effects=True, vmem_limit_bytes=60 << 20),
    )(*fields)
    return pl.pallas_call(
        hand_over,
        out_shape=shapes,
        in_specs=[pl.BlockSpec(memory_space=pl.ANY)] * 3,
        out_specs=[pl.BlockSpec(memory_space=pl.ANY)] * 3,
        scratch_shapes=[dma((3,))],
        compiler_params=pltpu.CompilerParams(vmem_limit_bytes=8 << 20),
    )(*found)


def solution(mesh):
    sizes = (mesh.shape["gz"], mesh.shape["gx"])
    in_specs = (P("gz", "gx", "gy"),) * 6 + (P("gx", "gy"),) * 2
    out_specs = (P("gz", "gx", "gy"),) * 3

    def step(
        electron_density, hole_density, potential, doping, electron_mobility, hole_mobility, cfl_map, fraction
    ):
        return tuple(
            on_device(
                sizes, electron_density, hole_density, electron_mobility, hole_mobility, potential, doping, cfl_map,
                fraction,
            )
        )

    return jax.shard_map(step, mesh=mesh, in_specs=in_specs, out_specs=out_specs, check_vma=False)
```
